256 devices in a mesh: gx: 4 (over x), gy: 8 (over z), vert: 8 (over y, core).
Axes of the slice: x: 4, y: 4, z: 8, core: 2. Of those that a mesh axis runs over, the one named last changes fastest.
Arguments:
- snapshot: float32 [16, 32, 1024, 1024], P('vert', None, 'gx', 'gy'), may hold values from -6 to 6
- basis_first: float32 [1024, 128], replicated, may hold values from -6 to 6
- basis_second: float32 [1024, 128], P('gy'), may hold values from -0.1875 to 0.1875
- basis_third: float32 [16, 32, 128], P('vert'), may hold values from -0.25 to 0.25
Outputs:
- basis_update: float32 [1024, 128], P('gx')
The draws below stay inside these ranges and needn't reach their ends.
All inputs are finite; a program needn't handle non-finite values.
Results may differ from the reference program's by a relative error of at most 0.00005.
Values sent between devices are 32-bit elements; how exact they have to be, the bound alone decides.
No kernel may reach another device: no remote copies, remote signals or barrier semaphores. Data moves between devices by JAX's collectives and lax.ppermute only.
A program may use at most 64 MiB of HBM per device.

```python
import jax
import jax.numpy as jnp
from jax import lax

VARS = 32
RANK = 128
NX = 1024
NY = 1024
NZ = 16


def block_scale(rng, dims, cuts, least, high):
    def one(dim, shards_of):
        heights = jax.random.uniform(jax.random.fold_in(jax.random.fold_in(rng, 6), dim), (shards_of,), jnp.float32, least / len(cuts), high / len(cuts))
        return jnp.repeat(jnp.exp(heights), dims[dim] // shards_of).reshape((-1,) + (1,) * (len(dims) - dim - 1))

    factor_of = one(*cuts[0])
    for cut in cuts[1:]:
        factor_of = factor_of * one(*cut)
    return factor_of


def centred(rng, dims, deviation, bound, cuts=(), dtype=jnp.bfloat16):
    result = jax.random.normal(rng, dims, jnp.float32) * deviation
    if len(cuts) > 0:
        result = block_scale(rng, dims, cuts, -0.22, 0.18) * result
    return jnp.clip(result, min=-bound, max=bound).astype(dtype)


def setup_inputs(seed: int = 0) -> dict:
    seeds = jax.random.split(jax.random.key(seed), 5)
    return {
        "snapshot": centred(seeds[0], (NZ, VARS, NX, NY), 1.0, 6.0, ((0, 8), (2, 4), (3, 8)), jnp.float32),
        "basis_first": centred(seeds[1], (NX, RANK), 1.0, 6.0, (), jnp.float32),
        "basis_second": centred(seeds[2], (NY, RANK), NY ** -0.5, 0.1875, ((0, 8),), jnp.float32),
        "basis_third": centred(seeds[3], (NZ, VARS, RANK), (NZ * VARS) ** -0.5, 0.25, ((0, 8),), jnp.float32),
    }


def reference(snapshot, basis_first, basis_second, basis_third):
    depth = NZ * VARS
    matrix_rows = snapshot.reshape(depth * NX, NY)
    partial_y = jnp.dot(matrix_rows, basis_second, precision=lax.Precision.HIGHEST, preferred_element_type=jnp.float32)
    partial_y = partial_y.reshape(depth, NX, RANK)
    third_mode = basis_third.reshape(depth, RANK).astype(jnp.float32)
    projected = jnp.einsum("kxr,kc->xrc", partial_y.astype(jnp.float32), third_mode, precision=lax.Precision.HIGHEST)
    unfolded = projected.reshape(NX, RANK * RANK)
    gram_matrix = jnp.dot(unfolded, unfolded.T, precision=lax.Precision.HIGHEST, preferred_element_type=jnp.float32)
    updated = jnp.dot(gram_matrix, basis_first, precision=lax.Precision.HIGHEST, preferred_element_type=jnp.float32)
    return updated / float(RANK * RANK)
```

```python
import functools

import jax
import jax.numpy as jnp
from jax import lax
from jax.experimental import pallas as pl
from jax.experimental.pallas import tpu as pltpu
from jax.sharding import PartitionSpec as P

HIGHEST = lax.Precision.HIGHEST
NT = (((1,), (1,)), ((), ()))
NN = (((1,), (0,)), ((), ()))
VMEM_LIMIT = 24 * 2**20
STEP = 8


def split(value):
    high = value.astype(jnp.bfloat16)
    return high, (value - high.astype(jnp.float32)).astype(jnp.bfloat16)


def product(high, both, value, dims):
    rows = high.shape[0]
    v_high, v_low = split(value)
    main = lax.dot_general(both, v_high, dims, preferred_element_type=jnp.float32)
    rest = lax.dot_general(high, v_low, dims, preferred_element_type=jnp.float32)
    return main[:rows] + (main[rows:] + rest)


def mode_kernel(second_ref, field_ref, out_ref):
    high, low = split(second_ref[...])
    both = jnp.concatenate([high, low], 0)
    for j in range(field_ref.shape[0]):
        out_ref[:, j, :] = product(high, both, field_ref[j], NT)


def mode_third_kernel(steps, second_ref, field_ref, third_ref, out_ref):
    @pl.when(pl.program_id(0) < steps)
    def _():
        mode_kernel(second_ref, field_ref, out_ref)

    @pl.when(pl.program_id(0) == steps)
    def _():
        rank = third_ref.shape[1]
        groups = third_ref.shape[0] // STEP
        for r in range(out_ref.shape[0]):
            g = r % groups
            out_ref[r, :, :rank] = third_ref[g * STEP : (g + 1) * STEP, :]


def mode_product(second, field, start, count, third=None):
    _, nx, ny = field.shape
    rows = second.shape[0]
    steps = count // STEP
    first = start // STEP
    kernel, extra, operands = mode_kernel, 0, (second, field)
    in_specs = [
        pl.BlockSpec((rows, ny), lambda i: (0, 0)),
        pl.BlockSpec((STEP, nx, ny), lambda i: (first + jnp.minimum(i, steps - 1), 0, 0)),
    ]
    if third is not None:
        kernel, extra, operands = functools.partial(mode_third_kernel, steps), 1, (second, field, third)
        in_specs.append(pl.BlockSpec(third.shape, lambda i: (0, 0)))
    return pl.pallas_call(
        kernel,
        grid=(steps + extra,),
        in_specs=in_specs,
        out_specs=pl.BlockSpec((rows, STEP, nx), lambda i: (0, i, 0)),
        out_shape=jax.ShapeDtypeStruct((rows, count + extra * STEP, nx), jnp.float32),
        compiler_params=pltpu.CompilerParams(vmem_limit_bytes=VMEM_LIMIT),
        cost_estimate=pl.CostEstimate(
            flops=6 * count * nx * ny * rows,
            bytes_accessed=4 * count * nx * (ny + rows),
            transcendentals=0,
        ),
    )(*operands)


def depth_kernel(third_ref, part_ref, out_ref):
    high, low = split(third_ref[...])
    both = jnp.concatenate([high, low], 0)
    n, _, depth, nx = part_ref.shape
    out_ref[0] = product(high, both, part_ref[...].reshape(n * depth, nx), NN)


def depth_product(third, part, depth):
    n, groups, _, nx = part.shape
    rank = third.shape[0]
    return pl.pallas_call(
        depth_kernel,
        grid=(groups,),
        in_specs=[
            pl.BlockSpec((rank, n * depth), lambda i: (0, 0)),
            pl.BlockSpec((n, 1, depth, nx), lambda i: (0, i, 0, 0)),
        ],
        out_specs=pl.BlockSpec((1, rank, nx), lambda i: (i, 0, 0)),
        out_shape=jax.ShapeDtypeStruct((groups, rank, nx), jnp.float32),
        compiler_params=pltpu.CompilerParams(vmem_limit_bytes=VMEM_LIMIT),
        cost_estimate=pl.CostEstimate(
            flops=6 * part.size * rank,
            bytes_accessed=4 * part.size,
            transcendentals=0,
        ),
    )(third, part)


def shifts(moves, axis):
    n = lax.axis_size(axis)
    values = lax.optimization_barrier([value for value, _ in moves])
    return [
        lax.ppermute(value, axis, [(i, (i + by) % n) for i in range(n)])
        for value, (_, by) in zip(values, moves)
    ]


def ring_sum(parts, axis):
    n = len(parts)
    half = n // 2
    mid = parts[half].shape[0] // 2
    up, down = shifts([(parts[half][:mid], 1), (parts[half][mid:], -1)], axis)
    for d in range(half - 1, 0, -1):
        if d == half - 1:
            up = jnp.concatenate([parts[d][:mid] + up, parts[d][mid:]], 0)
            down = jnp.concatenate([parts[n - d][:mid], parts[n - d][mid:] + down], 0)
        else:
            up = parts[d] + up
            down = parts[n - d] + down
        up, down = shifts([(up, 1), (down, -1)], axis)
    return parts[0] + up + down


def trade(value, axis):
    return lax.all_to_all(value, axis, 0, 0)


def spread(value, axis):
    n = lax.axis_size(axis)
    return trade(jnp.broadcast_to(value[None], (n,) + value.shape), axis)


def local(snapshot, basis_first, basis_second, basis_third):
    depth = snapshot.shape[0] * snapshot.shape[1]
    nx = snapshot.shape[2]
    ny = snapshot.shape[3]
    rank = basis_second.shape[1]
    gx = lax.axis_size("gx")
    gy = lax.axis_size("gy")
    vert = lax.axis_size("vert")
    share = rank // gy
    part_m = share // 2
    field = snapshot.reshape(depth, nx, ny)
    first = lax.dynamic_slice_in_dim(basis_first, lax.axis_index("gx") * nx, nx, 0)

    place = jnp.arange(rank // 2)
    ring = lax.axis_index("gy")
    order_m = (place // part_m + ring) % gy * share + place % part_m
    order_f = (place % gy + ring) % gy * share + part_m + place // gy

    def rows(order):
        turn = (order[:, None] == jnp.arange(rank)[None, :]).astype(jnp.float32)
        return lax.dot_general(turn, basis_second, NT, precision=HIGHEST)

    f = mode_product(rows(order_f), field, 0, depth, basis_third.reshape(depth, rank))
    f, rows_m = lax.optimization_barrier((f, rows(order_m)))
    f = trade(f.reshape(vert, gy, depth + STEP, nx), "vert")

    half = depth // 2
    m = []
    for start in (0, half):
        part = mode_product(rows_m, field, start, half).reshape(gy, part_m, half, nx)
        m.append(ring_sum([part[d] for d in range(gy)], "gy"))
    m, f = lax.optimization_barrier((jnp.concatenate(m, 1), f))
    m = trade(m, "vert")

    third = f[:, :, depth:, :rank].reshape(vert * depth, rank).T
    f = depth_product(third, f, depth)
    f = ring_sum([f[d] for d in range(gy)], "gy")
    f, m = lax.optimization_barrier((f, m))
    m = depth_product(third, m.reshape(vert, 1, depth, nx), depth)[0]

    columns = jnp.concatenate([f, m], 0)
    weights = jnp.dot(columns, first, precision=HIGHEST)
    others = shifts([(weights, d) for d in range(1, gx)], "gx")
    for other in others:
        weights = weights + other
    updated = lax.dot_general(columns, weights, (((0,), (0,)), ((), ())), precision=HIGHEST)

    updated = jnp.sum(trade(updated.reshape(vert, nx // vert, rank), "vert"), axis=0)
    updated = jnp.sum(spread(updated, "gy"), axis=0) / float(rank * rank)
    return spread(updated, "vert").reshape(nx, rank)


def solution(mesh):
    placed = (P("vert", None, "gx", "gy"), P(), P("gy", None), P("vert", None, None))
    return jax.shard_map(
        local, mesh=mesh, in_specs=placed, out_specs=P("gx", None), check_vma=False
    )
```

```python
import functools

import jax
import jax.numpy as jnp
import numpy as np
from jax import lax
from jax.experimental import pallas as pl
from jax.experimental.pallas import tpu as pltpu
from jax.sharding import PartitionSpec as P

HIGHEST = lax.Precision.HIGHEST
NT = (((1,), (1,)), ((), ()))
NN = (((1,), (0,)), ((), ()))
VMEM_LIMIT = 20 * 2**20
STEP = 8
SETS = 8
LANES = 4


def split(value):
    high = value.astype(jnp.bfloat16)
    return high, (value - high.astype(jnp.float32)).astype(jnp.bfloat16)


def product(high, both, value):
    rows = high.shape[0]
    v_high, v_low = split(value)
    main = lax.dot_general(both, v_high, NN, preferred_element_type=jnp.float32)
    rest = lax.dot_general(high, v_low, NN, preferred_element_type=jnp.float32)
    return main[:rows] + (main[rows:] + rest)


def mode_kernel(shapes, rolled, share, pick_ref, second_ref, third_ref, *refs):
    field_refs, refs = refs[:LANES], refs[LANES:]
    *out_refs, both_ref = refs
    rows, rank = pick_ref.shape
    ny = second_ref.shape[0]
    steps = pl.num_programs(0) - 1

    @pl.when(pl.program_id(0) == 0)
    def _():
        turned = pltpu.roll(pick_ref[:rolled, :], lax.axis_index("gy") * share, 1)
        pick = jnp.concatenate([turned, pick_ref[rolled:, :]], 0).astype(jnp.bfloat16)
        for part, value in enumerate(split(second_ref[...])):
            value = lax.dot_general(pick, value, NT, preferred_element_type=jnp.float32)
            both_ref[part * rows : (part + 1) * rows, :ny] = value.astype(jnp.bfloat16)
        both_ref[:rows, ny:] = both_ref[:rows, :ny]
        both_ref[rows:, ny:] = jnp.zeros((rows, ny), jnp.bfloat16)

    @pl.when(pl.program_id(0) < steps)
    def _():
        both = both_ref[...]
        for j in range(STEP):
            each = STEP // LANES
            pair = jnp.concatenate(split(field_refs[j // each][j % each]), 1)
            value = lax.dot_general(both, pair, NT, preferred_element_type=jnp.float32)
            value = value[:rows] + value[rows:]
            start = 0
            for (size, _), out_ref in zip(shapes, out_refs):
                out_ref[:, j, :] = value[start : start + size]
                start += size

    @pl.when(pl.program_id(0) == steps)
    def _():
        out_ref = out_refs[0]
        lanes = out_ref.shape[2] // rank
        tiles = third_ref.shape[0] // STEP
        groups = out_ref.shape[0] // SETS
        for r in range(out_ref.shape[0]):
            for lane in range(lanes):
                g = min(r % groups * lanes + lane, tiles - 1)
                out_ref[r, :, lane * rank : (lane + 1) * rank] = third_ref[g * STEP : (g + 1) * STEP, :]


def mode_product(picks, rolled, second, field, third, share):
    depth, nx, ny = field.shape
    steps = depth // STEP
    pick = np.concatenate(picks, 0)
    shapes = [(p.shape[0], depth) for p in picks]
    shapes[0] = (shapes[0][0], depth + STEP)
    rows, rank = pick.shape

    def last(i):
        return jnp.minimum(i, steps - 1)

    def piece(lane):
        return pl.BlockSpec((STEP // LANES, nx, ny), lambda i: (last(i) * LANES + lane, 0, 0))

    out_specs = [pl.BlockSpec((size, STEP, nx), lambda i: (0, last(i), 0)) for size, _ in shapes]
    out_specs[0] = pl.BlockSpec((shapes[0][0], STEP, nx), lambda i: (0, i, 0))
    return pl.pallas_call(
        functools.partial(mode_kernel, shapes, rolled, share),
        grid=(steps + 1,),
        in_specs=[
            pl.BlockSpec((rows, rank), lambda i: (0, 0)),
            pl.BlockSpec(second.shape, lambda i: (0, 0)),
            pl.BlockSpec(third.shape, lambda i: (0, 0)),
        ]
        + [piece(lane) for lane in range(LANES)],
        out_specs=out_specs,
        out_shape=[jax.ShapeDtypeStruct((*shape, nx), jnp.float32) for shape in shapes],
        scratch_shapes=[pltpu.VMEM((2 * rows, 2 * ny), jnp.bfloat16)],
        compiler_params=pltpu.CompilerParams(vmem_limit_bytes=58 * 2**20),
        cost_estimate=pl.CostEstimate(
            flops=6 * depth * nx * ny * rows,
            bytes_accessed=4 * depth * nx * (ny + rows),
            transcendentals=0,
        ),
    )(jnp.asarray(pick), second, third, *[field] * LANES)


def depth_kernel(third_ref, part_ref, out_ref, both_ref):
    rank = third_ref.shape[0]

    @pl.when(pl.program_id(0) == 0)
    def _():
        high, low = split(third_ref[...])
        both_ref[:rank] = high
        both_ref[rank:] = low

    n, groups, depth, nx = part_ref.shape
    for g in range(groups):
        value = part_ref[:, g].reshape(n * depth, nx)
        out_ref[g] = product(both_ref[:rank], both_ref[...], value)


def depth_product(third, part, depth):
    n, groups, _, nx = part.shape
    rank = third.shape[0]
    step = 2 if groups % 2 == 0 else 1
    return pl.pallas_call(
        depth_kernel,
        grid=(groups // step,),
        in_specs=[
            pl.BlockSpec((rank, n * depth), lambda i: (0, 0)),
            pl.BlockSpec((n, step, depth, nx), lambda i: (0, i, 0, 0)),
        ],
        out_specs=pl.BlockSpec((step, rank, nx), lambda i: (i, 0, 0)),
        out_shape=jax.ShapeDtypeStruct((groups, rank, nx), jnp.float32),
        scratch_shapes=[pltpu.VMEM((2 * rank, n * depth), jnp.bfloat16)],
        compiler_params=pltpu.CompilerParams(vmem_limit_bytes=VMEM_LIMIT),
        cost_estimate=pl.CostEstimate(
            flops=6 * n * groups * depth * nx * rank,
            bytes_accessed=4 * n * groups * depth * nx,
            transcendentals=0,
        ),
    )(third, part)


def after(value, other):
    return lax.optimization_barrier((value, other))[0]


def shifts(moves, axis):
    n = lax.axis_size(axis)
    values = lax.optimization_barrier([value for value, _ in moves])
    return [
        lax.ppermute(value, axis, [(i, (i + by) % n) for i in range(n)])
        for value, (_, by) in zip(values, moves)
    ]


def ring_steps(parts, axis, n):
    half = n // 2
    mid = parts[half].shape[0] // 2
    moving = shifts([(parts[half][:mid], 1), (parts[half][mid:], -1)], axis)
    for d in range(half - 1, 0, -1):
        up, down = yield moving
        if d == half - 1:
            up = jnp.concatenate([parts[d][:mid] + up, parts[d][mid:]], 0)
            down = jnp.concatenate([parts[n - d][:mid], parts[n - d][mid:] + down], 0)
        else:
            up = parts[d] + up
            down = parts[n - d] + down
        moving = shifts([(up, 1), (down, -1)], axis)
    up, down = yield moving
    yield parts[0] + up + down


def trade(value, axis):
    return lax.all_to_all(value, axis, 0, 0)


def spread(value, axis):
    n = lax.axis_size(axis)
    return trade(jnp.broadcast_to(value[None], (n,) + value.shape), axis)


def local(snapshot, basis_first, basis_second, basis_third):
    depth = snapshot.shape[0] * snapshot.shape[1]
    nx = snapshot.shape[2]
    ny = snapshot.shape[3]
    rank = basis_second.shape[1]
    gx = lax.axis_size("gx")
    gy = lax.axis_size("gy")
    vert = lax.axis_size("vert")
    share = rank // gy
    part_m = share // 2
    field = snapshot.reshape(depth, nx, ny)
    first = lax.dynamic_slice_in_dim(basis_first, lax.axis_index("gx") * nx, nx, 0)

    third = basis_third.reshape(depth, rank)

    half = gy // 2
    early = [(half + i) % gy for i in range(2 - half, half - 1)]
    late = [-1 % gy, 0, 1]

    def pick(pairs):
        return np.eye(rank, dtype=np.float32)[[place * share + within for place, within in pairs]]

    pick_1 = pick([(place, part_m + v) for v in range(vert) for place in early])
    pick_2 = pick([(place, part_m + v) for v in range(vert) for place in late])
    pick_m = pick([(place, within) for place in range(gy) for within in range(part_m)])

    picks = [pick_1, pick_2, pick_m]
    f1, f2, m = mode_product(picks, rank // 2, basis_second, field, third, share)
    f1 = trade(f1.reshape(vert, len(early), depth + STEP, nx), "vert")
    m = lax.psum_scatter(m, "gy", scatter_dimension=0, tiled=True)

    f1, f2 = lax.optimization_barrier((f1, f2))
    f2 = trade(f2.reshape(vert, len(late), depth, nx), "vert")
    third = f1[:, :, depth:].reshape(vert, len(early), STEP, nx // rank, rank)
    third = jnp.swapaxes(third, 2, 3).reshape(vert, -1, rank)[:, :depth].reshape(vert * depth, rank).T
    f1 = depth_product(third, f1, depth)
    parts = {place: f1[i] for i, place in enumerate(early)}
    ring_f = ring_steps(parts, "gy", gy)
    f = next(ring_f)
    for _ in range(half - 2):
        f = ring_f.send(f)

    f2 = after(f2, f)
    m = trade(after(m, f2), "vert")
    f2 = depth_product(third, f2, depth)
    parts.update({place: f2[i] for i, place in enumerate(late)})
    f = ring_f.send(f)
    m = depth_product(third, after(m, f).reshape(vert, 1, depth, nx), depth)[0]
    f = ring_f.send(f)

    columns = jnp.concatenate([f, m], 0)
    weights = jnp.dot(columns, first, precision=HIGHEST)
    others = shifts([(weights, d) for d in range(1, gx)], "gx")
    for other in others:
        weights = weights + other
    updated = lax.dot_general(columns, weights, (((0,), (0,)), ((), ())), precision=HIGHEST)

    updated = jnp.sum(trade(updated.reshape(vert, nx // vert, rank), "vert"), axis=0)
    updated = jnp.sum(spread(updated, "gy"), axis=0) / float(rank * rank)
    return spread(updated, "vert").reshape(nx, rank)


def solution(mesh):
    placed = (P("vert", None, "gx", "gy"), P(), P("gy", None), P("vert", None, None))
    return jax.shard_map(
        local, mesh=mesh, in_specs=placed, out_specs=P("gx", None), check_vma=False
    )
```

```python
import functools

import jax
import jax.numpy as jnp
import numpy as np
from jax import lax
from jax.experimental import pallas as pl
from jax.experimental.pallas import tpu as pltpu
from jax.sharding import PartitionSpec as P

HIGHEST = lax.Precision.HIGHEST
NT = (((1,), (1,)), ((), ()))
NN = (((1,), (0,)), ((), ()))
VMEM_LIMIT = 20 * 2**20
STEP = 8
SETS = 8


def split(value):
    high = value.astype(jnp.bfloat16)
    return high, (value - high.astype(jnp.float32)).astype(jnp.bfloat16)


def product(high, both, value):
    rows = high.shape[0]
    v_high, v_low = split(value)
    main = lax.dot_general(both, v_high, NN, preferred_element_type=jnp.float32)
    rest = lax.dot_general(high, v_low, NN, preferred_element_type=jnp.float32)
    return main[:rows] + (main[rows:] + rest)


def mode_kernel(roll, first, pick_ref, second_ref, field_ref, third_ref, out_ref, both_ref, held_ref, sems):
    rows, rank = pick_ref.shape
    ny = second_ref.shape[0]
    steps = held_ref.shape[0] // STEP

    def fetch(i):
        return pltpu.make_async_copy(
            field_ref.at[pl.ds((first + i) * STEP, STEP)], held_ref.at[pl.ds(i * STEP, STEP)], sems.at[i]
        )

    @pl.when(pl.program_id(0) == 0)
    def _():
        for i in range(steps):
            fetch(i).start()
        pick = pltpu.roll(pick_ref[...], lax.axis_index("gy") * roll, 1).astype(jnp.bfloat16)
        for part, value in enumerate(split(second_ref[...])):
            value = lax.dot_general(pick, value, NT, preferred_element_type=jnp.float32)
            both_ref[part * rows : (part + 1) * rows, :ny] = value.astype(jnp.bfloat16)
        both_ref[:rows, ny:] = both_ref[:rows, :ny]
        both_ref[rows:, ny:] = jnp.zeros((rows, ny), jnp.bfloat16)

    @pl.when(pl.program_id(0) < steps)
    def _():
        i = pl.program_id(0)
        fetch(i).wait()
        both = both_ref[...]
        for j in range(STEP):
            pair = jnp.concatenate(split(held_ref[i * STEP + j]), 1)
            value = lax.dot_general(both, pair, NT, preferred_element_type=jnp.float32)
            out_ref[:, j, :] = value[:rows] + value[rows:]

    if third_ref is None:
        return

    @pl.when(pl.program_id(0) == steps)
    def _():
        groups = out_ref.shape[0] // SETS
        for r in range(out_ref.shape[0]):
            g = r % groups
            out_ref[r, :, :rank] = third_ref[g * STEP : (g + 1) * STEP, :]
            out_ref[r, :, rank:] = third_ref[g * STEP : (g + 1) * STEP, :]


def plain_kernel(roll, first, pick_ref, second_ref, field_ref, *refs):
    mode_kernel(roll, first, pick_ref, second_ref, field_ref, None, *refs)


def mode_product(pick, second, field, roll, start, count, third=None):
    _, nx, ny = field.shape
    steps = count // STEP
    first = start // STEP
    rows, rank = pick.shape
    extra = 0 if third is None else 1

    in_specs = [
        pl.BlockSpec((rows, rank), lambda i: (0, 0)),
        pl.BlockSpec(second.shape, lambda i: (0, 0)),
        pl.BlockSpec(memory_space=pl.ANY),
    ]
    operands = [jnp.asarray(pick), second, field]
    if extra:
        in_specs.append(pl.BlockSpec(third.shape, lambda i: (0, 0)))
        operands.append(third)
    return pl.pallas_call(
        functools.partial(mode_kernel if extra else plain_kernel, roll, first),
        grid=(steps + extra,),
        in_specs=in_specs,
        out_specs=pl.BlockSpec((rows, STEP, nx), lambda i: (0, i, 0)),
        out_shape=jax.ShapeDtypeStruct((rows, count + extra * STEP, nx), jnp.float32),
        scratch_shapes=[
            pltpu.VMEM((2 * rows, 2 * ny), jnp.bfloat16),
            pltpu.VMEM((count, nx, ny), jnp.float32),
            pltpu.SemaphoreType.DMA((steps,)),
        ],
        compiler_params=pltpu.CompilerParams(vmem_limit_bytes=54 * 2**20),
        cost_estimate=pl.CostEstimate(
            flops=6 * count * nx * ny * rows,
            bytes_accessed=4 * count * nx * (ny + rows),
            transcendentals=0,
        ),
    )(*operands)


def depth_kernel(third_ref, part_ref, out_ref, both_ref):
    rank = third_ref.shape[0]

    @pl.when(pl.program_id(0) == 0)
    def _():
        high, low = split(third_ref[...])
        both_ref[:rank] = high
        both_ref[rank:] = low

    n, groups, depth, nx = part_ref.shape
    for g in range(groups):
        value = part_ref[:, g].reshape(n * depth, nx)
        out_ref[g] = product(both_ref[:rank], both_ref[...], value)


def depth_product(third, part, depth):
    n, groups, _, nx = part.shape
    rank = third.shape[0]
    step = 2 if groups % 2 == 0 else 1
    return pl.pallas_call(
        depth_kernel,
        grid=(groups // step,),
        in_specs=[
            pl.BlockSpec((rank, n * depth), lambda i: (0, 0)),
            pl.BlockSpec((n, step, depth, nx), lambda i: (0, i, 0, 0)),
        ],
        out_specs=pl.BlockSpec((step, rank, nx), lambda i: (i, 0, 0)),
        out_shape=jax.ShapeDtypeStruct((groups, rank, nx), jnp.float32),
        scratch_shapes=[pltpu.VMEM((2 * rank, n * depth), jnp.bfloat16)],
        compiler_params=pltpu.CompilerParams(vmem_limit_bytes=VMEM_LIMIT),
        cost_estimate=pl.CostEstimate(
            flops=6 * n * groups * depth * nx * rank,
            bytes_accessed=4 * n * groups * depth * nx,
            transcendentals=0,
        ),
    )(third, part)


def after(value, other):
    return lax.optimization_barrier((value, other))[0]


def shifts(moves, axis):
    n = lax.axis_size(axis)
    values = lax.optimization_barrier([value for value, _ in moves])
    return [
        lax.ppermute(value, axis, [(i, (i + by) % n) for i in range(n)])
        for value, (_, by) in zip(values, moves)
    ]


def ring_sum(parts, axis):
    n = len(parts)
    half = n // 2
    mid = parts[half].shape[0] // 2
    up, down = shifts([(parts[half][:mid], 1), (parts[half][mid:], -1)], axis)
    for d in range(half - 1, 0, -1):
        if d == half - 1:
            up = jnp.concatenate([parts[d][:mid] + up, parts[d][mid:]], 0)
            down = jnp.concatenate([parts[n - d][:mid], parts[n - d][mid:] + down], 0)
        else:
            up = parts[d] + up
            down = parts[n - d] + down
        up, down = shifts([(up, 1), (down, -1)], axis)
    return parts[0] + up + down


def trade(value, axis):
    return lax.all_to_all(value, axis, 0, 0)


def spread(value, axis):
    n = lax.axis_size(axis)
    return trade(jnp.broadcast_to(value[None], (n,) + value.shape), axis)


def local(snapshot, basis_first, basis_second, basis_third):
    depth = snapshot.shape[0] * snapshot.shape[1]
    nx = snapshot.shape[2]
    ny = snapshot.shape[3]
    rank = basis_second.shape[1]
    gx = lax.axis_size("gx")
    gy = lax.axis_size("gy")
    vert = lax.axis_size("vert")
    share = rank // gy
    part_m = share // 2
    field = snapshot.reshape(depth, nx, ny)
    first = lax.dynamic_slice_in_dim(basis_first, lax.axis_index("gx") * nx, nx, 0)

    third = basis_third.reshape(depth, rank)

    def pick(pairs):
        return np.eye(rank, dtype=np.float32)[[place * share + within for place, within in pairs]]

    pick_f = pick([(place, part_m + v) for v in range(vert) for place in range(gy)])
    pick_m = pick([(place, within) for place in range(gy) for within in range(part_m)])

    f = mode_product(pick_f, basis_second, field, share, 0, depth, third)
    second = after(basis_second, f)
    f = trade(f.reshape(vert, gy, depth + STEP, nx), "vert")

    half = depth // 2
    m = []
    for start in (0, half):
        part = mode_product(pick_m, second, field, share, start, half)
        m.append(ring_sum([part[d * part_m : (d + 1) * part_m] for d in range(gy)], "gy"))
    m, f = lax.optimization_barrier((jnp.concatenate(m, 1), f))
    m = trade(m, "vert")

    third = f[:, :, depth:, :rank].reshape(vert * depth, rank).T
    f = depth_product(third, f, depth)
    f = ring_sum([f[d] for d in range(gy)], "gy")
    f, m = lax.optimization_barrier((f, m))
    m = depth_product(third, m.reshape(vert, 1, depth, nx), depth)[0]

    columns = jnp.concatenate([f, m], 0)
    weights = jnp.dot(columns, first, precision=HIGHEST)
    others = shifts([(weights, d) for d in range(1, gx)], "gx")
    for other in others:
        weights = weights + other
    updated = lax.dot_general(columns, weights, (((0,), (0,)), ((), ())), precision=HIGHEST)

    updated = jnp.sum(trade(updated.reshape(vert, nx // vert, rank), "vert"), axis=0)
    updated = jnp.sum(spread(updated, "gy"), axis=0) / float(rank * rank)
    return spread(updated, "vert").reshape(nx, rank)


def solution(mesh):
    placed = (P("vert", None, "gx", "gy"), P(), P("gy", None), P("vert", None, None))
    return jax.shard_map(
        local, mesh=mesh, in_specs=placed, out_specs=P("gx", None), check_vma=False
    )
```

```python
import functools

import jax
import jax.numpy as jnp
import numpy as np
from jax import lax
from jax.experimental import pallas as pl
from jax.experimental.pallas import tpu as pltpu
from jax.sharding import PartitionSpec as P

HIGHEST = lax.Precision.HIGHEST
NT = (((1,), (1,)), ((), ()))
NN = (((1,), (0,)), ((), ()))
VMEM_LIMIT = 20 * 2**20
STEP = 8
SETS = 8


def split(value):
    high = value.astype(jnp.bfloat16)
    return high, (value - high.astype(jnp.float32)).astype(jnp.bfloat16)


def product(high, both, value):
    rows = high.shape[0]
    v_high, v_low = split(value)
    main = lax.dot_general(both, v_high, NN, preferred_element_type=jnp.float32)
    rest = lax.dot_general(high, v_low, NN, preferred_element_type=jnp.float32)
    return main[:rows] + (main[rows:] + rest)


def mode_kernel(roll, first, halves, pick_ref, second_ref, field_ref, *refs):
    count = len(halves)
    third_ref, refs = (refs[0], refs[1:]) if len(refs) > count + 3 else (None, refs)
    out_refs, (both_ref, held_ref, sems) = refs[:count], refs[count:]
    rows = pick_ref.shape[0] // count
    ny = second_ref.shape[0]
    steps = held_ref.shape[0] // STEP

    def fetch(i):
        return pltpu.make_async_copy(
            field_ref.at[pl.ds((first + i) * STEP, STEP)], held_ref.at[pl.ds(i * STEP, STEP)], sems.at[i]
        )

    @pl.when(pl.program_id(0) == 0)
    def _():
        for i in range(steps):
            fetch(i).start()
        pick = pltpu.roll(pick_ref[...], lax.axis_index("gy") * roll, 1).astype(jnp.bfloat16)
        both_ref[...] = jnp.zeros_like(both_ref)
        for part, value in enumerate(split(second_ref[...])):
            value = lax.dot_general(pick, value, NT, preferred_element_type=jnp.float32).astype(jnp.bfloat16)
            for n in range(count):
                place = (2 * n + part) * rows
                both_ref[place : place + rows, :ny] = value[n * rows : (n + 1) * rows]
                if part == 0:
                    both_ref[place : place + rows, ny:] = value[n * rows : (n + 1) * rows]

    def multiply(outs):
        i = pl.program_id(0)
        fetch(i).wait()
        both = both_ref[: 2 * rows * len(outs)]
        for j in range(STEP):
            pair = jnp.concatenate(split(held_ref[i * STEP + j]), 1)
            value = lax.dot_general(both, pair, NT, preferred_element_type=jnp.float32)
            for n, out_ref in enumerate(outs):
                base = 2 * n * rows
                out_ref[:, j, :] = value[base : base + rows] + value[base + rows : base + 2 * rows]

    if any(halves):

        @pl.when(pl.program_id(0) < steps // 2)
        def _():
            multiply(out_refs)

        @pl.when((pl.program_id(0) >= steps // 2) & (pl.program_id(0) < steps))
        def _():
            multiply([out_ref for out_ref, half in zip(out_refs, halves) if not half])

    else:

        @pl.when(pl.program_id(0) < steps)
        def _():
            multiply(out_refs)

    if third_ref is None:
        return

    @pl.when(pl.program_id(0) == steps)
    def _():
        out_ref = out_refs[0]
        rank = third_ref.shape[1]
        groups = out_ref.shape[0] // SETS
        for r in range(out_ref.shape[0]):
            g = r % groups
            out_ref[r, :, :rank] = third_ref[g * STEP : (g + 1) * STEP, :]
            out_ref[r, :, rank:] = third_ref[g * STEP : (g + 1) * STEP, :]


def mode_product(picks, halves, second, field, roll, start, count, third=None):
    _, nx, ny = field.shape
    steps = count // STEP
    first = start // STEP
    pick = np.concatenate(picks, 0)
    rows = picks[0].shape[0]
    extra = 0 if third is None else 1
    planes = [count // 2 if half else count for half in halves]
    planes[0] += extra * STEP

    def out(size):
        return pl.BlockSpec((rows, STEP, nx), lambda i: (0, jnp.minimum(i, size // STEP - 1), 0))

    in_specs = [
        pl.BlockSpec(pick.shape, lambda i: (0, 0)),
        pl.BlockSpec(second.shape, lambda i: (0, 0)),
        pl.BlockSpec(memory_space=pl.ANY),
    ]
    operands = [jnp.asarray(pick), second, field]
    if extra:
        in_specs.append(pl.BlockSpec(third.shape, lambda i: (0, 0)))
        operands.append(third)
    return pl.pallas_call(
        functools.partial(mode_kernel, roll, first, halves),
        grid=(steps + extra,),
        in_specs=in_specs,
        out_specs=[out(size) for size in planes],
        out_shape=[jax.ShapeDtypeStruct((rows, size, nx), jnp.float32) for size in planes],
        scratch_shapes=[
            pltpu.VMEM((2 * pick.shape[0], 2 * ny), jnp.bfloat16),
            pltpu.VMEM((count, nx, ny), jnp.float32),
            pltpu.SemaphoreType.DMA((steps,)),
        ],
        compiler_params=pltpu.CompilerParams(vmem_limit_bytes=54 * 2**20),
        cost_estimate=pl.CostEstimate(
            flops=6 * count * nx * ny * pick.shape[0],
            bytes_accessed=4 * count * nx * (ny + pick.shape[0]),
            transcendentals=0,
        ),
    )(*operands)


def depth_kernel(third_ref, part_ref, out_ref, both_ref):
    rank = third_ref.shape[3]

    @pl.when(pl.program_id(0) == 0)
    def _():
        high, low = split(third_ref[...].reshape(-1, rank).T)
        both_ref[:rank] = high
        both_ref[rank:] = low

    n, groups, depth, nx = part_ref.shape
    for g in range(groups):
        value = part_ref[:, g].reshape(n * depth, nx)
        out_ref[g] = product(both_ref[:rank], both_ref[...], value)


def depth_product(gathered, part, rank):
    n, tiles, planes, _ = gathered.shape
    _, groups, _, nx = part.shape
    depth = planes - STEP
    step = 2 if groups % 2 == 0 else 1
    return pl.pallas_call(
        depth_kernel,
        grid=(groups // step,),
        in_specs=[
            pl.BlockSpec((n, tiles, STEP, rank), lambda i: (0, 0, depth // STEP, 0)),
            pl.BlockSpec((n, step, depth, nx), lambda i: (0, i, 0, 0)),
        ],
        out_specs=pl.BlockSpec((step, rank, nx), lambda i: (i, 0, 0)),
        out_shape=jax.ShapeDtypeStruct((groups, rank, nx), jnp.float32),
        scratch_shapes=[pltpu.VMEM((2 * rank, n * depth), jnp.bfloat16)],
        compiler_params=pltpu.CompilerParams(vmem_limit_bytes=VMEM_LIMIT),
        cost_estimate=pl.CostEstimate(
            flops=6 * n * groups * depth * nx * rank,
            bytes_accessed=4 * n * groups * depth * nx,
            transcendentals=0,
        ),
    )(gathered, part)


def after(value, other):
    return lax.optimization_barrier((value, other))[0]


def shifts(moves, axis):
    n = lax.axis_size(axis)
    values = lax.optimization_barrier([value for value, _ in moves])
    return [
        lax.ppermute(value, axis, [(i, (i + by) % n) for i in range(n)])
        for value, (_, by) in zip(values, moves)
    ]


def ring_steps(parts, axis):
    n = len(parts)
    half = n // 2
    mid = parts[half].shape[0] // 2
    moving = shifts([(parts[half][:mid], 1), (parts[half][mid:], -1)], axis)
    for d in range(half - 1, 0, -1):
        up, down = yield moving
        if d == half - 1:
            up = jnp.concatenate([parts[d][:mid] + up, parts[d][mid:]], 0)
            down = jnp.concatenate([parts[n - d][:mid], parts[n - d][mid:] + down], 0)
        else:
            up = parts[d] + up
            down = parts[n - d] + down
        moving = shifts([(up, 1), (down, -1)], axis)
    up, down = yield moving
    yield parts[0] + up + down


def ring_sum(parts, axis):
    steps = ring_steps(parts, axis)
    value = next(steps)
    for _ in range(len(parts) // 2):
        value = steps.send(value)
    return value


def trade(value, axis):
    return lax.all_to_all(value, axis, 0, 0)


def spread(value, axis):
    n = lax.axis_size(axis)
    return trade(jnp.broadcast_to(value[None], (n,) + value.shape), axis)


def local(snapshot, basis_first, basis_second, basis_third):
    depth = snapshot.shape[0] * snapshot.shape[1]
    nx = snapshot.shape[2]
    ny = snapshot.shape[3]
    rank = basis_second.shape[1]
    gx = lax.axis_size("gx")
    gy = lax.axis_size("gy")
    vert = lax.axis_size("vert")
    share = rank // gy
    part_m = share // 2
    field = snapshot.reshape(depth, nx, ny)
    first = lax.dynamic_slice_in_dim(basis_first, lax.axis_index("gx") * nx, nx, 0)

    third = basis_third.reshape(depth, rank)

    def pick(pairs):
        return np.eye(rank, dtype=np.float32)[[place * share + within for place, within in pairs]]

    pick_f = pick([(place, part_m + v) for v in range(vert) for place in range(gy)])
    pick_m = pick([(place, within) for place in range(gy) for within in range(part_m)])

    half = depth // 2
    f, m1 = mode_product([pick_f, pick_m], (False, True), basis_second, field, share, 0, depth, third)
    second = after(basis_second, f)
    f = trade(f.reshape(vert, gy, depth + STEP, nx), "vert")

    (m2,) = mode_product([pick_m], (False,), second, field, share, half, half)
    m = [ring_sum([part[d * part_m : (d + 1) * part_m] for d in range(gy)], "gy") for part in (m1, m2)]
    m, f = lax.optimization_barrier((jnp.concatenate(m, 1), f))
    m = trade(m, "vert")

    parts = depth_product(f, f, rank)
    ring = ring_steps([parts[d] for d in range(gy)], "gy")
    moving = next(ring)
    for _ in range(gy // 2 - 2):
        moving = ring.send(moving)
    moving, m = lax.optimization_barrier((moving, m))
    m = depth_product(f, m.reshape(vert, 1, depth, nx), rank)[0]
    f = ring.send(ring.send(moving))

    columns = jnp.concatenate([f, m], 0)
    weights = jnp.dot(columns, first, precision=HIGHEST)
    others = shifts([(weights, d) for d in range(1, gx)], "gx")
    for other in others:
        weights = weights + other
    updated = lax.dot_general(columns, weights, (((0,), (0,)), ((), ())), precision=HIGHEST)

    updated = jnp.sum(trade(updated.reshape(vert, nx // vert, rank), "vert"), axis=0)
    updated = jnp.sum(spread(updated, "gy"), axis=0) / float(rank * rank)
    return spread(updated, "vert").reshape(nx, rank)


def solution(mesh):
    placed = (P("vert", None, "gx", "gy"), P(), P("gy", None), P("vert", None, None))
    return jax.shard_map(
        local, mesh=mesh, in_specs=placed, out_specs=P("gx", None), check_vma=False
    )
```

```python
import functools

import jax
import jax.numpy as jnp
import numpy as np
from jax import lax
from jax.experimental import pallas as pl
from jax.experimental.pallas import tpu as pltpu
from jax.sharding import PartitionSpec as P

HIGHEST = lax.Precision.HIGHEST
NT = (((1,), (1,)), ((), ()))
NN = (((1,), (0,)), ((), ()))
VMEM_LIMIT = 8 * 2**20
STEP = 8
SETS = 8


def split(value):
    high = value.astype(jnp.bfloat16)
    return high, (value - high.astype(jnp.float32)).astype(jnp.bfloat16)


def product(high, both, value):
    rows = high.shape[0]
    v_high, v_low = split(value)
    main = lax.dot_general(both, v_high, NN, preferred_element_type=jnp.float32)
    rest = lax.dot_general(high, v_low, NN, preferred_element_type=jnp.float32)
    return main[:rows] + (main[rows:] + rest)


def mode_kernel(roll, first, halves, pick_ref, second_ref, field_ref, *refs):
    count = len(halves)
    third_ref, refs = (refs[0], refs[1:]) if len(refs) > count + 3 else (None, refs)
    out_refs, (both_ref, held_ref, sems) = refs[:count], refs[count:]
    rows = pick_ref.shape[0] // count
    ny = second_ref.shape[0]
    steps = held_ref.shape[0] // STEP

    def fetch(i):
        return pltpu.make_async_copy(
            field_ref.at[pl.ds((first + i) * STEP, STEP)], held_ref.at[pl.ds(i * STEP, STEP)], sems.at[i]
        )

    @pl.when(pl.program_id(0) == 0)
    def _():
        for i in range(steps):
            fetch(i).start()
        pick = pltpu.roll(pick_ref[...], lax.axis_index("gy") * roll, 1).astype(jnp.bfloat16)
        both_ref[...] = jnp.zeros_like(both_ref)
        for part, value in enumerate(split(second_ref[...])):
            value = lax.dot_general(pick, value, NT, preferred_element_type=jnp.float32).astype(jnp.bfloat16)
            for n in range(count):
                place = (2 * n + part) * rows
                both_ref[place : place + rows, :ny] = value[n * rows : (n + 1) * rows]
                if part == 0:
                    both_ref[place : place + rows, ny:] = value[n * rows : (n + 1) * rows]

    def multiply(outs):
        i = pl.program_id(0)
        fetch(i).wait()
        both = both_ref[: 2 * rows * len(outs)]
        for j in range(STEP):
            pair = jnp.concatenate(split(held_ref[i * STEP + j]), 1)
            value = lax.dot_general(both, pair, NT, preferred_element_type=jnp.float32)
            for n, out_ref in enumerate(outs):
                base = 2 * n * rows
                out_ref[:, j, :] = value[base : base + rows] + value[base + rows : base + 2 * rows]

    if any(halves):

        @pl.when(pl.program_id(0) < steps // 2)
        def _():
            multiply(out_refs)

        @pl.when((pl.program_id(0) >= steps // 2) & (pl.program_id(0) < steps))
        def _():
            multiply([out_ref for out_ref, half in zip(out_refs, halves) if not half])

    else:

        @pl.when(pl.program_id(0) < steps)
        def _():
            multiply(out_refs)

    if third_ref is None:
        return

    @pl.when(pl.program_id(0) == steps)
    def _():
        out_ref = out_refs[0]
        rank = third_ref.shape[1]
        groups = out_ref.shape[0] // SETS
        for r in range(out_ref.shape[0]):
            g = r % groups
            out_ref[r, :, :rank] = third_ref[g * STEP : (g + 1) * STEP, :]
            out_ref[r, :, rank:] = third_ref[g * STEP : (g + 1) * STEP, :]


def mode_product(picks, halves, second, field, roll, start, count, limit, third=None):
    _, nx, ny = field.shape
    steps = count // STEP
    first = start // STEP
    pick = np.concatenate(picks, 0)
    rows = picks[0].shape[0]
    extra = 0 if third is None else 1
    planes = [count // 2 if half else count for half in halves]
    planes[0] += extra * STEP

    def out(size):
        return pl.BlockSpec((rows, STEP, nx), lambda i: (0, jnp.minimum(i, size // STEP - 1), 0))

    in_specs = [
        pl.BlockSpec(pick.shape, lambda i: (0, 0)),
        pl.BlockSpec(second.shape, lambda i: (0, 0)),
        pl.BlockSpec(memory_space=pl.ANY),
    ]
    operands = [jnp.asarray(pick), second, field]
    if extra:
        in_specs.append(pl.BlockSpec(third.shape, lambda i: (0, 0)))
        operands.append(third)
    return pl.pallas_call(
        functools.partial(mode_kernel, roll, first, halves),
        grid=(steps + extra,),
        in_specs=in_specs,
        out_specs=[out(size) for size in planes],
        out_shape=[jax.ShapeDtypeStruct((rows, size, nx), jnp.float32) for size in planes],
        scratch_shapes=[
            pltpu.VMEM((2 * pick.shape[0], 2 * ny), jnp.bfloat16),
            pltpu.VMEM((count, nx, ny), jnp.float32),
            pltpu.SemaphoreType.DMA((steps,)),
        ],
        compiler_params=pltpu.CompilerParams(vmem_limit_bytes=limit * 2**20),
        cost_estimate=pl.CostEstimate(
            flops=6 * count * nx * ny * pick.shape[0],
            bytes_accessed=4 * count * nx * (ny + pick.shape[0]),
            transcendentals=0,
        ),
    )(*operands)


def depth_kernel(third_ref, part_ref, out_ref, both_ref):
    rank = third_ref.shape[3]

    @pl.when(pl.program_id(0) == 0)
    def _():
        high, low = split(third_ref[...].reshape(-1, rank).T)
        both_ref[:rank] = high
        both_ref[rank:] = low

    n, groups, depth, nx = part_ref.shape
    for g in range(groups):
        value = part_ref[:, g].reshape(n * depth, nx)
        out_ref[g] = product(both_ref[:rank], both_ref[...], value)


def depth_product(gathered, part, rank):
    n, tiles, planes, _ = gathered.shape
    _, groups, _, nx = part.shape
    depth = planes - STEP
    step = 2 if groups % 2 == 0 else 1
    return pl.pallas_call(
        depth_kernel,
        grid=(groups // step,),
        in_specs=[
            pl.BlockSpec((n, tiles, STEP, rank), lambda i: (0, 0, depth // STEP, 0)),
            pl.BlockSpec((n, step, depth, nx), lambda i: (0, i, 0, 0)),
        ],
        out_specs=pl.BlockSpec((step, rank, nx), lambda i: (i, 0, 0)),
        out_shape=jax.ShapeDtypeStruct((groups, rank, nx), jnp.float32),
        scratch_shapes=[pltpu.VMEM((2 * rank, n * depth), jnp.bfloat16)],
        compiler_params=pltpu.CompilerParams(vmem_limit_bytes=VMEM_LIMIT),
        cost_estimate=pl.CostEstimate(
            flops=6 * n * groups * depth * nx * rank,
            bytes_accessed=4 * n * groups * depth * nx,
            transcendentals=0,
        ),
    )(gathered, part)


def shifts(moves, axis):
    n = lax.axis_size(axis)
    values = lax.optimization_barrier([value for value, _ in moves])
    return [
        lax.ppermute(value, axis, [(i, (i + by) % n) for i in range(n)])
        for value, (_, by) in zip(values, moves)
    ]


def ring_steps(parts, axis):
    n = len(parts)
    half = n // 2
    mid = parts[half].shape[0] // 2
    moving = shifts([(parts[half][:mid], 1), (parts[half][mid:], -1)], axis)
    for d in range(half - 1, 0, -1):
        up, down = yield moving
        if d == half - 1:
            up = jnp.concatenate([parts[d][:mid] + up, parts[d][mid:]], 0)
            down = jnp.concatenate([parts[n - d][:mid], parts[n - d][mid:] + down], 0)
        else:
            up = parts[d] + up
            down = parts[n - d] + down
        moving = shifts([(up, 1), (down, -1)], axis)
    up, down = yield moving
    yield parts[0] + up + down


def ring_sum(parts, axis):
    steps = ring_steps(parts, axis)
    value = next(steps)
    for _ in range(len(parts) // 2):
        value = steps.send(value)
    return value


def trade(value, axis):
    return lax.all_to_all(value, axis, 0, 0)


def spread(value, axis):
    n = lax.axis_size(axis)
    return trade(jnp.broadcast_to(value[None], (n,) + value.shape), axis)


def local(snapshot, basis_first, basis_second, basis_third):
    depth = snapshot.shape[0] * snapshot.shape[1]
    nx = snapshot.shape[2]
    ny = snapshot.shape[3]
    rank = basis_second.shape[1]
    gx = lax.axis_size("gx")
    gy = lax.axis_size("gy")
    vert = lax.axis_size("vert")
    share = rank // gy
    part_m = share // 2
    field = snapshot.reshape(depth, nx, ny)
    first = lax.dynamic_slice_in_dim(basis_first, lax.axis_index("gx") * nx, nx, 0)

    third = basis_third.reshape(depth, rank)

    def pick(pairs):
        return np.eye(rank, dtype=np.float32)[[place * share + within for place, within in pairs]]

    pick_f = pick([(place, part_m + v) for v in range(vert) for place in range(gy)])
    pick_m = pick([(place, within) for place in range(gy) for within in range(part_m)])

    half = depth // 2
    f, m1 = mode_product([pick_f, pick_m], (False, True), basis_second, field, share, 0, depth, 54, third)
    second, f = lax.optimization_barrier((basis_second, f))
    f = trade(f.reshape(vert, gy, depth + STEP, nx), "vert")

    (m2,) = mode_product([pick_m], (False,), second, field, share, half, half, 46)
    m = [ring_sum([part[d * part_m : (d + 1) * part_m] for d in range(gy)], "gy") for part in (m1, m2)]
    m, f = lax.optimization_barrier((jnp.concatenate(m, 1), f))
    m = trade(m, "vert")

    parts = depth_product(f, f, rank)
    ring = ring_steps([parts[d] for d in range(gy)], "gy")
    moving = next(ring)
    for _ in range(gy // 2 - 2):
        moving = ring.send(moving)
    moving, m = lax.optimization_barrier((moving, m))
    m = depth_product(f, m.reshape(vert, 1, depth, nx), rank)[0]
    f = ring.send(ring.send(moving))

    columns = jnp.concatenate([f, m], 0)
    weights = jnp.dot(columns, first, precision=HIGHEST)
    others = shifts([(weights, d) for d in range(1, gx)], "gx")
    for other in others:
        weights = weights + other
    updated = lax.dot_general(columns, weights, (((0,), (0,)), ((), ())), precision=HIGHEST)

    updated = jnp.sum(trade(updated.reshape(vert, nx // vert, rank), "vert"), axis=0)
    updated = jnp.sum(spread(updated, "gy"), axis=0) / float(rank * rank)
    return spread(updated, "vert").reshape(nx, rank)


def solution(mesh):
    placed = (P("vert", None, "gx", "gy"), P(), P("gy", None), P("vert", None, None))
    return jax.shard_map(
        local, mesh=mesh, in_specs=placed, out_specs=P("gx", None), check_vma=False
    )
```

```python
import functools

import jax
import jax.numpy as jnp
import numpy as np
from jax import lax
from jax.experimental import pallas as pl
from jax.experimental.pallas import tpu as pltpu
from jax.sharding import PartitionSpec as P

HIGHEST = lax.Precision.HIGHEST
NT = (((1,), (1,)), ((), ()))
NN = (((1,), (0,)), ((), ()))
VMEM_LIMIT = 10 * 2**20
STEP = 8
SETS = 8


def split(value):
    high = value.astype(jnp.bfloat16)
    return high, (value - high.astype(jnp.float32)).astype(jnp.bfloat16)


def product(high, both, value):
    rows = high.shape[0]
    v_high, v_low = split(value)
    main = lax.dot_general(both, v_high, NN, preferred_element_type=jnp.float32)
    rest = lax.dot_general(high, v_low, NN, preferred_element_type=jnp.float32)
    return main[:rows] + (main[rows:] + rest)


def mode_kernel(roll, first, pick_ref, second_ref, field_ref, out_ref, both_ref, held_ref, sems):
    rows = pick_ref.shape[0]
    ny = second_ref.shape[0]
    steps = held_ref.shape[0] // STEP
    now = pl.program_id(0)

    def fetch(i):
        return pltpu.make_async_copy(
            field_ref.at[pl.ds((first + i) * STEP, STEP)], held_ref.at[pl.ds(i * STEP, STEP)], sems.at[i]
        )

    @pl.when(now == 0)
    def _():
        for i in range(steps):
            fetch(i).start()
        pick = pltpu.roll(pick_ref[...], lax.axis_index("gy") * roll, 1).astype(jnp.bfloat16)
        both_ref[...] = jnp.zeros_like(both_ref)
        for part, value in enumerate(split(second_ref[...])):
            value = lax.dot_general(pick, value, NT, preferred_element_type=jnp.float32).astype(jnp.bfloat16)
            both_ref[part * rows : (part + 1) * rows, :ny] = value
            if part == 0:
                both_ref[:rows, ny:] = value

    fetch(now).wait()
    both = both_ref[...]
    for j in range(STEP):
        pair = jnp.concatenate(split(held_ref[now * STEP + j]), 1)
        value = lax.dot_general(both, pair, NT, preferred_element_type=jnp.float32)
        out_ref[:, j, :] = value[:rows] + value[rows:]


def mode_product(pick, second, field, roll, start, count):
    _, nx, ny = field.shape
    steps = count // STEP
    rows = pick.shape[0]
    return pl.pallas_call(
        functools.partial(mode_kernel, roll, start // STEP),
        grid=(steps,),
        in_specs=[
            pl.BlockSpec(pick.shape, lambda i: (0, 0)),
            pl.BlockSpec(second.shape, lambda i: (0, 0)),
            pl.BlockSpec(memory_space=pl.ANY),
        ],
        out_specs=pl.BlockSpec((rows, STEP, nx), lambda i: (0, i, 0)),
        out_shape=jax.ShapeDtypeStruct((rows, count, nx), jnp.float32),
        scratch_shapes=[
            pltpu.VMEM((2 * rows, 2 * ny), jnp.bfloat16),
            pltpu.VMEM((count, nx, ny), jnp.float32),
            pltpu.SemaphoreType.DMA((steps,)),
        ],
        compiler_params=pltpu.CompilerParams(vmem_limit_bytes=46 * 2**20),
        cost_estimate=pl.CostEstimate(
            flops=6 * count * nx * ny * rows,
            bytes_accessed=4 * count * nx * (ny + rows),
            transcendentals=0,
        ),
    )(jnp.asarray(pick), second, field)


def lead_kernel(
    roll, pick_ref, second_ref, third_ref, field_ref, f_ref, m_ref, both_ref, held_ref, stage_ref, pack_ref, sems, out_sems, third_sem
):
    rows = pick_ref.shape[0] // 2
    ny = second_ref.shape[0]
    rank = third_ref.shape[1]
    steps = held_ref.shape[0] // STEP
    sets = f_ref.shape[0]
    groups = rows // sets
    per_half = steps // 2
    now = pl.program_id(0)

    def fetch(i):
        return pltpu.make_async_copy(
            field_ref.at[pl.ds(i * STEP, STEP)], held_ref.at[pl.ds(i * STEP, STEP)], sems.at[i]
        )

    def send(i):
        plane = pl.multiple_of(i % per_half * STEP, STEP)
        target = f_ref.at[:, pl.ds(i // per_half * groups, groups), pl.ds(plane, STEP), :]
        return pltpu.make_async_copy(stage_ref.at[i % 2], target, out_sems.at[i % 2])

    def send_third(v):
        return pltpu.make_async_copy(pack_ref, f_ref.at[v, 2 * groups], third_sem.at[v])

    @pl.when(now == 0)
    def _():
        for i in range(steps):
            fetch(i).start()
        for half in range(2):
            pack_ref[:, half * rank : (half + 1) * rank] = third_ref[half * per_half * STEP : (half + 1) * per_half * STEP, :]
        for v in range(sets):
            send_third(v).start()
        pick = pltpu.roll(pick_ref[...], lax.axis_index("gy") * roll, 1).astype(jnp.bfloat16)
        both_ref[...] = jnp.zeros_like(both_ref)
        for part, value in enumerate(split(second_ref[...])):
            value = lax.dot_general(pick, value, NT, preferred_element_type=jnp.float32).astype(jnp.bfloat16)
            for n in range(2):
                place = (2 * n + part) * rows
                both_ref[place : place + rows, :ny] = value[n * rows : (n + 1) * rows]
                if part == 0:
                    both_ref[place : place + rows, ny:] = value[n * rows : (n + 1) * rows]

    @pl.when(now >= 2)
    def _():
        send(now - 2).wait()

    fetch(now).wait()

    def multiply(with_m):
        both = both_ref[...] if with_m else both_ref[: 2 * rows]
        for j in range(STEP):
            pair = jnp.concatenate(split(held_ref[now * STEP + j]), 1)
            value = lax.dot_general(both, pair, NT, preferred_element_type=jnp.float32)
            f = value[:rows] + value[rows : 2 * rows]
            for v in range(sets):
                stage_ref[now % 2, v, :, j, :] = f[v * groups : (v + 1) * groups]
            if with_m:
                m_ref[:, j, :] = value[2 * rows : 3 * rows] + value[3 * rows :]

    @pl.when(now < per_half)
    def _():
        multiply(True)

    @pl.when(now >= per_half)
    def _():
        multiply(False)

    send(now).start()

    @pl.when(now == steps - 1)
    def _():
        send(now - 1).wait()
        send(now).wait()
        for v in range(sets):
            send_third(v).wait()


def lead_product(pick_f, pick_m, second, field, roll, third):
    depth, nx, ny = field.shape
    steps = depth // STEP
    pick = np.concatenate([pick_f, pick_m], 0)
    rows = pick_f.shape[0]
    groups = rows // SETS
    return pl.pallas_call(
        functools.partial(lead_kernel, roll),
        grid=(steps,),
        in_specs=[
            pl.BlockSpec(pick.shape, lambda i: (0, 0)),
            pl.BlockSpec(second.shape, lambda i: (0, 0)),
            pl.BlockSpec(third.shape, lambda i: (0, 0)),
            pl.BlockSpec(memory_space=pl.ANY),
        ],
        out_specs=[
            pl.BlockSpec(memory_space=pl.ANY),
            pl.BlockSpec((rows, STEP, nx), lambda i: (0, jnp.minimum(i, steps // 2 - 1), 0)),
        ],
        out_shape=[
            jax.ShapeDtypeStruct((SETS, 2 * groups + 1, depth // 2, nx), jnp.float32),
            jax.ShapeDtypeStruct((rows, depth // 2, nx), jnp.float32),
        ],
        scratch_shapes=[
            pltpu.VMEM((4 * rows, 2 * ny), jnp.bfloat16),
            pltpu.VMEM((depth, nx, ny), jnp.float32),
            pltpu.VMEM((2, SETS, groups, STEP, nx), jnp.float32),
            pltpu.VMEM((depth // 2, nx), jnp.float32),
            pltpu.SemaphoreType.DMA((steps,)),
            pltpu.SemaphoreType.DMA((2,)),
            pltpu.SemaphoreType.DMA((SETS,)),
        ],
        compiler_params=pltpu.CompilerParams(vmem_limit_bytes=54 * 2**20),
        cost_estimate=pl.CostEstimate(
            flops=6 * depth * nx * ny * pick.shape[0],
            bytes_accessed=4 * depth * nx * (ny + pick.shape[0]),
            transcendentals=0,
        ),
    )(jnp.asarray(pick), second, third, field)


def depth_kernel(third_ref, one_ref, two_ref, out_ref, both_ref):
    rank, nx = out_ref.shape[1:]

    @pl.when(pl.program_id(0) == 0)
    def _():
        halves = [third_ref[:, 0, :, half * rank : (half + 1) * rank].reshape(-1, rank) for half in range(2)]
        high, low = split(jnp.concatenate(halves, 0).T)
        both_ref[:rank] = high
        both_ref[rank:] = low

    for g in range(out_ref.shape[0]):
        value = jnp.concatenate([ref[:, g].reshape(-1, nx) for ref in (one_ref, two_ref)], 0)
        out_ref[g] = product(both_ref[:rank], both_ref[...], value)


def depth_product(gathered, part, rank, groups):
    n, count, planes, nx = gathered.shape
    step = 2 if groups % 2 == 0 else 1
    block = (n, step, planes, nx)
    return pl.pallas_call(
        depth_kernel,
        grid=(groups // step,),
        in_specs=[
            pl.BlockSpec((n, 1, planes, nx), lambda i: (0, count - 1, 0, 0)),
            pl.BlockSpec(block, lambda i: (0, i, 0, 0)),
            pl.BlockSpec(block, lambda i: (0, groups // step + i, 0, 0)),
        ],
        out_specs=pl.BlockSpec((step, rank, nx), lambda i: (i, 0, 0)),
        out_shape=jax.ShapeDtypeStruct((groups, rank, nx), jnp.float32),
        scratch_shapes=[pltpu.VMEM((2 * rank, 2 * n * planes), jnp.bfloat16)],
        compiler_params=pltpu.CompilerParams(vmem_limit_bytes=VMEM_LIMIT),
        cost_estimate=pl.CostEstimate(
            flops=12 * n * groups * planes * nx * rank,
            bytes_accessed=8 * n * groups * planes * nx,
            transcendentals=0,
        ),
    )(gathered, part, part)


def shifts(moves, axis):
    n = lax.axis_size(axis)
    values = lax.optimization_barrier([value for value, _ in moves])
    return [
        lax.ppermute(value, axis, [(i, (i + by) % n) for i in range(n)])
        for value, (_, by) in zip(values, moves)
    ]


def ring_steps(parts, axis):
    n = len(parts)
    half = n // 2
    mid = parts[half].shape[0] // 2
    moving = shifts([(parts[half][:mid], 1), (parts[half][mid:], -1)], axis)
    for d in range(half - 1, 0, -1):
        up, down = yield moving
        if d == half - 1:
            up = jnp.concatenate([parts[d][:mid] + up, parts[d][mid:]], 0)
            down = jnp.concatenate([parts[n - d][:mid], parts[n - d][mid:] + down], 0)
        else:
            up = parts[d] + up
            down = parts[n - d] + down
        moving = shifts([(up, 1), (down, -1)], axis)
    up, down = yield moving
    yield parts[0] + up + down


def ring_sum(parts, axis):
    steps = ring_steps(parts, axis)
    value = next(steps)
    for _ in range(len(parts) // 2):
        value = steps.send(value)
    return value


def trade(value, axis):
    return lax.all_to_all(value, axis, 0, 0)


def spread(value, axis):
    n = lax.axis_size(axis)
    return trade(jnp.broadcast_to(value[None], (n,) + value.shape), axis)


def local(snapshot, basis_first, basis_second, basis_third):
    depth = snapshot.shape[0] * snapshot.shape[1]
    nx = snapshot.shape[2]
    ny = snapshot.shape[3]
    rank = basis_second.shape[1]
    gx = lax.axis_size("gx")
    gy = lax.axis_size("gy")
    vert = lax.axis_size("vert")
    share = rank // gy
    part_m = share // 2
    field = snapshot.reshape(depth, nx, ny)
    first = lax.dynamic_slice_in_dim(basis_first, lax.axis_index("gx") * nx, nx, 0)

    third = basis_third.reshape(depth, rank)

    def pick(pairs):
        return np.eye(rank, dtype=np.float32)[[place * share + within for place, within in pairs]]

    pick_f = pick([(place, part_m + v) for v in range(vert) for place in range(gy)])
    pick_m = pick([(place, within) for place in range(gy) for within in range(part_m)])

    half = depth // 2
    f, m1 = lead_product(pick_f, pick_m, basis_second, field, share, third)
    second, f = lax.optimization_barrier((basis_second, f))
    f = trade(f, "vert")

    m2 = mode_product(pick_m, second, field, share, half, half)
    m = [ring_sum([part[d * part_m : (d + 1) * part_m] for d in range(gy)], "gy") for part in (m1, m2)]
    m, f = lax.optimization_barrier((jnp.concatenate(m, 1), f))
    m = trade(m, "vert")

    parts = depth_product(f, f, rank, gy)
    ring = ring_steps([parts[d] for d in range(gy)], "gy")
    moving = next(ring)
    for _ in range(gy // 2 - 2):
        moving = ring.send(moving)
    moving, m = lax.optimization_barrier((moving, m))
    m = depth_product(f, m.reshape(vert, 2, half, nx), rank, 1)[0]
    f = ring.send(ring.send(moving))

    columns = jnp.concatenate([f, m], 0)
    weights = jnp.dot(columns, first, precision=HIGHEST)
    others = shifts([(weights, d) for d in range(1, gx)], "gx")
    for other in others:
        weights = weights + other
    updated = lax.dot_general(columns, weights, (((0,), (0,)), ((), ())), precision=HIGHEST)

    updated = jnp.sum(trade(updated.reshape(vert, nx // vert, rank), "vert"), axis=0)
    updated = jnp.sum(spread(updated, "gy"), axis=0) / float(rank * rank)
    return spread(updated, "vert").reshape(nx, rank)


def solution(mesh):
    placed = (P("vert", None, "gx", "gy"), P(), P("gy", None), P("vert", None, None))
    return jax.shard_map(
        local, mesh=mesh, in_specs=placed, out_specs=P("gx", None), check_vma=False
    )
```

```python
import functools

import jax
import jax.numpy as jnp
import numpy as np
from jax import lax
from jax.experimental import pallas as pl
from jax.experimental.pallas import tpu as pltpu
from jax.sharding import PartitionSpec as P

HIGHEST = lax.Precision.HIGHEST
NT = (((1,), (1,)), ((), ()))
NN = (((1,), (0,)), ((), ()))
VMEM_LIMIT = 10 * 2**20
STEP = 8
AHEAD = 3
SETS = 8


def split(value):
    high = value.astype(jnp.bfloat16)
    return high, (value - high.astype(jnp.float32)).astype(jnp.bfloat16)


def product(high, both, value):
    rows = high.shape[0]
    v_high, v_low = split(value)
    main = lax.dot_general(both, v_high, NN, preferred_element_type=jnp.float32)
    rest = lax.dot_general(high, v_low, NN, preferred_element_type=jnp.float32)
    return main[:rows] + (main[rows:] + rest)


def mode_kernel(roll, first, pick_ref, second_ref, field_ref, out_ref, both_ref, held_ref, sems):
    rows = pick_ref.shape[0]
    ny = second_ref.shape[0]
    steps = held_ref.shape[0] // STEP
    now = pl.program_id(0)

    def fetch(i):
        return pltpu.make_async_copy(
            field_ref.at[pl.ds((first + i) * STEP, STEP)], held_ref.at[pl.ds(i * STEP, STEP)], sems.at[i]
        )

    @pl.when(now == 0)
    def _():
        for i in range(AHEAD):
            fetch(i).start()
        pick = pltpu.roll(pick_ref[...], lax.axis_index("gy") * roll, 1).astype(jnp.bfloat16)
        both_ref[...] = jnp.zeros_like(both_ref)
        for part, value in enumerate(split(second_ref[...])):
            value = lax.dot_general(pick, value, NT, preferred_element_type=jnp.float32).astype(jnp.bfloat16)
            both_ref[part * rows : (part + 1) * rows, :ny] = value
            if part == 0:
                both_ref[:rows, ny:] = value

    @pl.when(now + AHEAD < steps)
    def _():
        fetch(now + AHEAD).start()

    fetch(now).wait()
    both = both_ref[...]
    for j in range(STEP):
        pair = jnp.concatenate(split(held_ref[now * STEP + j]), 1)
        value = lax.dot_general(both, pair, NT, preferred_element_type=jnp.float32)
        out_ref[:, j, :] = value[:rows] + value[rows:]


def mode_product(pick, second, field, roll, start, count):
    _, nx, ny = field.shape
    steps = count // STEP
    rows = pick.shape[0]
    return pl.pallas_call(
        functools.partial(mode_kernel, roll, start // STEP),
        grid=(steps,),
        in_specs=[
            pl.BlockSpec(pick.shape, lambda i: (0, 0)),
            pl.BlockSpec(second.shape, lambda i: (0, 0)),
            pl.BlockSpec(memory_space=pl.ANY),
        ],
        out_specs=pl.BlockSpec((rows, STEP, nx), lambda i: (0, i, 0)),
        out_shape=jax.ShapeDtypeStruct((rows, count, nx), jnp.float32),
        scratch_shapes=[
            pltpu.VMEM((2 * rows, 2 * ny), jnp.bfloat16),
            pltpu.VMEM((count, nx, ny), jnp.float32),
            pltpu.SemaphoreType.DMA((steps,)),
        ],
        compiler_params=pltpu.CompilerParams(vmem_limit_bytes=46 * 2**20),
        cost_estimate=pl.CostEstimate(
            flops=6 * count * nx * ny * rows,
            bytes_accessed=4 * count * nx * (ny + rows),
            transcendentals=0,
        ),
    )(jnp.asarray(pick), second, field)


def lead_kernel(
    roll, pick_ref, second_ref, third_ref, field_ref, f_ref, m_ref, both_ref, held_ref, stage_ref, pack_ref, sems, out_sems, third_sem
):
    rows = pick_ref.shape[0] // 2
    ny = second_ref.shape[0]
    rank = third_ref.shape[1]
    steps = held_ref.shape[0] // STEP
    sets = f_ref.shape[0]
    groups = rows // sets
    per_half = steps // 2
    now = pl.program_id(0)

    def fetch(i):
        return pltpu.make_async_copy(
            field_ref.at[pl.ds(i * STEP, STEP)], held_ref.at[pl.ds(i * STEP, STEP)], sems.at[i]
        )

    def send(i):
        plane = pl.multiple_of(i % per_half * STEP, STEP)
        target = f_ref.at[:, pl.ds(i // per_half * groups, groups), pl.ds(plane, STEP), :]
        return pltpu.make_async_copy(stage_ref.at[i % 2], target, out_sems.at[i % 2])

    def send_third(v):
        return pltpu.make_async_copy(pack_ref, f_ref.at[v, 2 * groups], third_sem.at[v])

    @pl.when(now == 0)
    def _():
        for i in range(AHEAD):
            fetch(i).start()
        for half in range(2):
            pack_ref[:, half * rank : (half + 1) * rank] = third_ref[half * per_half * STEP : (half + 1) * per_half * STEP, :]
        for v in range(sets):
            send_third(v).start()
        pick = pltpu.roll(pick_ref[...], lax.axis_index("gy") * roll, 1).astype(jnp.bfloat16)
        both_ref[...] = jnp.zeros_like(both_ref)
        for part, value in enumerate(split(second_ref[...])):
            value = lax.dot_general(pick, value, NT, preferred_element_type=jnp.float32).astype(jnp.bfloat16)
            for n in range(2):
                place = (2 * n + part) * rows
                both_ref[place : place + rows, :ny] = value[n * rows : (n + 1) * rows]
                if part == 0:
                    both_ref[place : place + rows, ny:] = value[n * rows : (n + 1) * rows]

    @pl.when(now >= 2)
    def _():
        send(now - 2).wait()

    @pl.when(now + AHEAD < steps)
    def _():
        fetch(now + AHEAD).start()

    fetch(now).wait()

    def multiply(with_m):
        both = both_ref[...] if with_m else both_ref[: 2 * rows]
        for j in range(STEP):
            pair = jnp.concatenate(split(held_ref[now * STEP + j]), 1)
            value = lax.dot_general(both, pair, NT, preferred_element_type=jnp.float32)
            f = value[:rows] + value[rows : 2 * rows]
            for v in range(sets):
                stage_ref[now % 2, v, :, j, :] = f[v * groups : (v + 1) * groups]
            if with_m:
                m_ref[:, j, :] = value[2 * rows : 3 * rows] + value[3 * rows :]

    @pl.when(now < per_half)
    def _():
        multiply(True)

    @pl.when(now >= per_half)
    def _():
        multiply(False)

    send(now).start()

    @pl.when(now == steps - 1)
    def _():
        send(now - 1).wait()
        send(now).wait()
        for v in range(sets):
            send_third(v).wait()


def lead_product(pick_f, pick_m, second, field, roll, third):
    depth, nx, ny = field.shape
    steps = depth // STEP
    pick = np.concatenate([pick_f, pick_m], 0)
    rows = pick_f.shape[0]
    groups = rows // SETS
    return pl.pallas_call(
        functools.partial(lead_kernel, roll),
        grid=(steps,),
        in_specs=[
            pl.BlockSpec(pick.shape, lambda i: (0, 0)),
            pl.BlockSpec(second.shape, lambda i: (0, 0)),
            pl.BlockSpec(third.shape, lambda i: (0, 0)),
            pl.BlockSpec(memory_space=pl.ANY),
        ],
        out_specs=[
            pl.BlockSpec(memory_space=pl.ANY),
            pl.BlockSpec((rows, STEP, nx), lambda i: (0, jnp.minimum(i, steps // 2 - 1), 0)),
        ],
        out_shape=[
            jax.ShapeDtypeStruct((SETS, 2 * groups + 1, depth // 2, nx), jnp.float32),
            jax.ShapeDtypeStruct((rows, depth // 2, nx), jnp.float32),
        ],
        scratch_shapes=[
            pltpu.VMEM((4 * rows, 2 * ny), jnp.bfloat16),
            pltpu.VMEM((depth, nx, ny), jnp.float32),
            pltpu.VMEM((2, SETS, groups, STEP, nx), jnp.float32),
            pltpu.VMEM((depth // 2, nx), jnp.float32),
            pltpu.SemaphoreType.DMA((steps,)),
            pltpu.SemaphoreType.DMA((2,)),
            pltpu.SemaphoreType.DMA((SETS,)),
        ],
        compiler_params=pltpu.CompilerParams(vmem_limit_bytes=54 * 2**20),
        cost_estimate=pl.CostEstimate(
            flops=6 * depth * nx * ny * pick.shape[0],
            bytes_accessed=4 * depth * nx * (ny + pick.shape[0]),
            transcendentals=0,
        ),
    )(jnp.asarray(pick), second, third, field)


def depth_kernel(third_ref, part_ref, out_ref, both_ref, held_ref, sems):
    rank, nx = out_ref.shape[1:]
    groups = held_ref.shape[0]
    now = pl.program_id(0)

    def fetch(g, half):
        return pltpu.make_async_copy(part_ref.at[:, half * groups + g], held_ref.at[g, half], sems.at[g, half])

    @pl.when(now == 0)
    def _():
        for g in range(min(AHEAD, groups)):
            for half in range(2):
                fetch(g, half).start()
        halves = [third_ref[:, 0, :, half * rank : (half + 1) * rank].reshape(-1, rank) for half in range(2)]
        high, low = split(jnp.concatenate(halves, 0).T)
        both_ref[:rank] = high
        both_ref[rank:] = low

    @pl.when(now + AHEAD < groups)
    def _():
        for half in range(2):
            fetch(now + AHEAD, half).start()

    for half in range(2):
        fetch(now, half).wait()
    out_ref[0] = product(both_ref[:rank], both_ref[...], held_ref[now].reshape(-1, nx))


def depth_product(gathered, part, rank, groups):
    n, count, planes, nx = gathered.shape
    return pl.pallas_call(
        depth_kernel,
        grid=(groups,),
        in_specs=[
            pl.BlockSpec((n, 1, planes, nx), lambda i: (0, count - 1, 0, 0)),
            pl.BlockSpec(memory_space=pl.ANY),
        ],
        out_specs=pl.BlockSpec((1, rank, nx), lambda i: (i, 0, 0)),
        out_shape=jax.ShapeDtypeStruct((groups, rank, nx), jnp.float32),
        scratch_shapes=[
            pltpu.VMEM((2 * rank, 2 * n * planes), jnp.bfloat16),
            pltpu.VMEM((groups, 2, n, planes, nx), jnp.float32),
            pltpu.SemaphoreType.DMA((groups, 2)),
        ],
        compiler_params=pltpu.CompilerParams(vmem_limit_bytes=VMEM_LIMIT),
        cost_estimate=pl.CostEstimate(
            flops=12 * n * groups * planes * nx * rank,
            bytes_accessed=8 * n * groups * planes * nx,
            transcendentals=0,
        ),
    )(gathered, part)


def shifts(moves, axis):
    n = lax.axis_size(axis)
    values = lax.optimization_barrier([value for value, _ in moves])
    return [
        lax.ppermute(value, axis, [(i, (i + by) % n) for i in range(n)])
        for value, (_, by) in zip(values, moves)
    ]


def ring_steps(parts, axis):
    n = len(parts)
    half = n // 2
    mid = parts[half].shape[0] // 2
    moving = shifts([(parts[half][:mid], 1), (parts[half][mid:], -1)], axis)
    for d in range(half - 1, 0, -1):
        up, down = yield moving
        if d == half - 1:
            up = jnp.concatenate([parts[d][:mid] + up, parts[d][mid:]], 0)
            down = jnp.concatenate([parts[n - d][:mid], parts[n - d][mid:] + down], 0)
        else:
            up = parts[d] + up
            down = parts[n - d] + down
        moving = shifts([(up, 1), (down, -1)], axis)
    up, down = yield moving
    yield parts[0] + up + down


def ring_sum(parts, axis):
    steps = ring_steps(parts, axis)
    value = next(steps)
    for _ in range(len(parts) // 2):
        value = steps.send(value)
    return value


def trade(value, axis):
    return lax.all_to_all(value, axis, 0, 0)


def spread(value, axis):
    n = lax.axis_size(axis)
    return trade(jnp.broadcast_to(value[None], (n,) + value.shape), axis)


def local(snapshot, basis_first, basis_second, basis_third):
    depth = snapshot.shape[0] * snapshot.shape[1]
    nx = snapshot.shape[2]
    ny = snapshot.shape[3]
    rank = basis_second.shape[1]
    gx = lax.axis_size("gx")
    gy = lax.axis_size("gy")
    vert = lax.axis_size("vert")
    share = rank // gy
    part_m = share // 2
    field = snapshot.reshape(depth, nx, ny)
    first = lax.dynamic_slice_in_dim(basis_first, lax.axis_index("gx") * nx, nx, 0)

    third = basis_third.reshape(depth, rank)

    def pick(pairs):
        return np.eye(rank, dtype=np.float32)[[place * share + within for place, within in pairs]]

    pick_f = pick([(place, part_m + v) for v in range(vert) for place in range(gy)])
    pick_m = pick([(place, within) for place in range(gy) for within in range(part_m)])

    half = depth // 2
    f, m1 = lead_product(pick_f, pick_m, basis_second, field, share, third)
    second, f = lax.optimization_barrier((basis_second, f))
    f = trade(f, "vert")

    m2 = mode_product(pick_m, second, field, share, half, half)
    m = [ring_sum([part[d * part_m : (d + 1) * part_m] for d in range(gy)], "gy") for part in (m1, m2)]
    m, f = lax.optimization_barrier((jnp.concatenate(m, 1), f))
    m = trade(m, "vert")

    parts = depth_product(f, f, rank, gy)
    ring = ring_steps([parts[d] for d in range(gy)], "gy")
    moving = next(ring)
    for _ in range(gy // 2 - 2):
        moving = ring.send(moving)
    moving, m = lax.optimization_barrier((moving, m))
    m = depth_product(f, m.reshape(vert, 2, half, nx), rank, 1)[0]
    f = ring.send(ring.send(moving))

    columns = jnp.concatenate([f, m], 0)
    weights = jnp.dot(columns, first, precision=HIGHEST)
    others = shifts([(weights, d) for d in range(1, gx)], "gx")
    for other in others:
        weights = weights + other
    updated = lax.dot_general(columns, weights, (((0,), (0,)), ((), ())), precision=HIGHEST)

    updated = jnp.sum(trade(updated.reshape(vert, nx // vert, rank), "vert"), axis=0)
    updated = jnp.sum(spread(updated, "gy"), axis=0) / float(rank * rank)
    return spread(updated, "vert").reshape(nx, rank)


def solution(mesh):
    placed = (P("vert", None, "gx", "gy"), P(), P("gy", None), P("vert", None, None))
    return jax.shard_map(
        local, mesh=mesh, in_specs=placed, out_specs=P("gx", None), check_vma=False
    )
```

```python
import functools

import jax
import jax.numpy as jnp
import numpy as np
from jax import lax
from jax.experimental import pallas as pl
from jax.experimental.pallas import tpu as pltpu
from jax.sharding import PartitionSpec as P

HIGHEST = lax.Precision.HIGHEST
NT = (((1,), (1,)), ((), ()))
NN = (((1,), (0,)), ((), ()))
VMEM_LIMIT = 10 * 2**20
STEP = 16
SETS = 8


def split(value):
    high = value.astype(jnp.bfloat16)
    return high, (value - high.astype(jnp.float32)).astype(jnp.bfloat16)


def product(high, both, value):
    rows = high.shape[0]
    v_high, v_low = split(value)
    main = lax.dot_general(both, v_high, NN, preferred_element_type=jnp.float32)
    rest = lax.dot_general(high, v_low, NN, preferred_element_type=jnp.float32)
    return main[:rows] + (main[rows:] + rest)


def mode_kernel(roll, first, pick_ref, second_ref, field_ref, out_ref, both_ref, held_ref, sems):
    rows = pick_ref.shape[0]
    ny = second_ref.shape[0]
    steps = held_ref.shape[0] // STEP
    now = pl.program_id(0)

    def fetch(i):
        return pltpu.make_async_copy(
            field_ref.at[pl.ds((first + i) * STEP, STEP)], held_ref.at[pl.ds(i * STEP, STEP)], sems.at[i]
        )

    @pl.when(now == 0)
    def _():
        for i in range(steps):
            fetch(i).start()
        pick = pltpu.roll(pick_ref[...], lax.axis_index("gy") * roll, 1).astype(jnp.bfloat16)
        both_ref[...] = jnp.zeros_like(both_ref)
        for part, value in enumerate(split(second_ref[...])):
            value = lax.dot_general(pick, value, NT, preferred_element_type=jnp.float32).astype(jnp.bfloat16)
            both_ref[part * rows : (part + 1) * rows, :ny] = value
            if part == 0:
                both_ref[:rows, ny:] = value

    fetch(now).wait()
    both = both_ref[...]
    for j in range(STEP):
        pair = jnp.concatenate(split(held_ref[now * STEP + j]), 1)
        value = lax.dot_general(both, pair, NT, preferred_element_type=jnp.float32)
        out_ref[:, j, :] = value[:rows] + value[rows:]


def mode_product(pick, second, field, roll, start, count):
    _, nx, ny = field.shape
    steps = count // STEP
    rows = pick.shape[0]
    return pl.pallas_call(
        functools.partial(mode_kernel, roll, start // STEP),
        grid=(steps,),
        in_specs=[
            pl.BlockSpec(pick.shape, lambda i: (0, 0)),
            pl.BlockSpec(second.shape, lambda i: (0, 0)),
            pl.BlockSpec(memory_space=pl.ANY),
        ],
        out_specs=pl.BlockSpec((rows, STEP, nx), lambda i: (0, i, 0)),
        out_shape=jax.ShapeDtypeStruct((rows, count, nx), jnp.float32),
        scratch_shapes=[
            pltpu.VMEM((2 * rows, 2 * ny), jnp.bfloat16),
            pltpu.VMEM((count, nx, ny), jnp.float32),
            pltpu.SemaphoreType.DMA((steps,)),
        ],
        compiler_params=pltpu.CompilerParams(vmem_limit_bytes=46 * 2**20),
        cost_estimate=pl.CostEstimate(
            flops=6 * count * nx * ny * rows,
            bytes_accessed=4 * count * nx * (ny + rows),
            transcendentals=0,
        ),
    )(jnp.asarray(pick), second, field)


def lead_kernel(
    roll, pick_ref, second_ref, third_ref, field_ref, f_ref, m_ref, both_ref, held_ref, stage_ref, pack_ref, sems, out_sems, third_sem
):
    rows = pick_ref.shape[0] // 2
    ny = second_ref.shape[0]
    rank = third_ref.shape[1]
    steps = held_ref.shape[0] // STEP
    sets = f_ref.shape[0]
    groups = rows // sets
    per_half = steps // 2
    now = pl.program_id(0)

    def fetch(i):
        return pltpu.make_async_copy(
            field_ref.at[pl.ds(i * STEP, STEP)], held_ref.at[pl.ds(i * STEP, STEP)], sems.at[i]
        )

    def send(i):
        plane = pl.multiple_of(i % per_half * STEP, STEP)
        target = f_ref.at[:, pl.ds(i // per_half * groups, groups), pl.ds(plane, STEP), :]
        return pltpu.make_async_copy(stage_ref.at[i % 2], target, out_sems.at[i % 2])

    def send_third(v):
        return pltpu.make_async_copy(pack_ref, f_ref.at[v, 2 * groups], third_sem.at[v])

    @pl.when(now == 0)
    def _():
        for i in range(steps):
            fetch(i).start()
        for half in range(2):
            pack_ref[:, half * rank : (half + 1) * rank] = third_ref[half * per_half * STEP : (half + 1) * per_half * STEP, :]
        for v in range(sets):
            send_third(v).start()
        pick = pltpu.roll(pick_ref[...], lax.axis_index("gy") * roll, 1).astype(jnp.bfloat16)
        both_ref[...] = jnp.zeros_like(both_ref)
        for part, value in enumerate(split(second_ref[...])):
            value = lax.dot_general(pick, value, NT, preferred_element_type=jnp.float32).astype(jnp.bfloat16)
            for n in range(2):
                place = (2 * n + part) * rows
                both_ref[place : place + rows, :ny] = value[n * rows : (n + 1) * rows]
                if part == 0:
                    both_ref[place : place + rows, ny:] = value[n * rows : (n + 1) * rows]

    @pl.when(now >= 2)
    def _():
        send(now - 2).wait()

    fetch(now).wait()

    def multiply(with_m):
        both = both_ref[...] if with_m else both_ref[: 2 * rows]
        for j in range(STEP):
            pair = jnp.concatenate(split(held_ref[now * STEP + j]), 1)
            value = lax.dot_general(both, pair, NT, preferred_element_type=jnp.float32)
            f = value[:rows] + value[rows : 2 * rows]
            for v in range(sets):
                stage_ref[now % 2, v, :, j, :] = f[v * groups : (v + 1) * groups]
            if with_m:
                m_ref[:, j, :] = value[2 * rows : 3 * rows] + value[3 * rows :]

    @pl.when(now < per_half)
    def _():
        multiply(True)

    @pl.when(now >= per_half)
    def _():
        multiply(False)

    send(now).start()

    @pl.when(now == steps - 1)
    def _():
        send(now - 1).wait()
        send(now).wait()
        for v in range(sets):
            send_third(v).wait()


def lead_product(pick_f, pick_m, second, field, roll, third):
    depth, nx, ny = field.shape
    steps = depth // STEP
    pick = np.concatenate([pick_f, pick_m], 0)
    rows = pick_f.shape[0]
    groups = rows // SETS
    return pl.pallas_call(
        functools.partial(lead_kernel, roll),
        grid=(steps,),
        in_specs=[
            pl.BlockSpec(pick.shape, lambda i: (0, 0)),
            pl.BlockSpec(second.shape, lambda i: (0, 0)),
            pl.BlockSpec(third.shape, lambda i: (0, 0)),
            pl.BlockSpec(memory_space=pl.ANY),
        ],
        out_specs=[
            pl.BlockSpec(memory_space=pl.ANY),
            pl.BlockSpec((rows, STEP, nx), lambda i: (0, jnp.minimum(i, steps // 2 - 1), 0)),
        ],
        out_shape=[
            jax.ShapeDtypeStruct((SETS, 2 * groups + 1, depth // 2, nx), jnp.float32),
            jax.ShapeDtypeStruct((rows, depth // 2, nx), jnp.float32),
        ],
        scratch_shapes=[
            pltpu.VMEM((4 * rows, 2 * ny), jnp.bfloat16),
            pltpu.VMEM((depth, nx, ny), jnp.float32),
            pltpu.VMEM((2, SETS, groups, STEP, nx), jnp.float32),
            pltpu.VMEM((depth // 2, nx), jnp.float32),
            pltpu.SemaphoreType.DMA((steps,)),
            pltpu.SemaphoreType.DMA((2,)),
            pltpu.SemaphoreType.DMA((SETS,)),
        ],
        compiler_params=pltpu.CompilerParams(vmem_limit_bytes=54 * 2**20),
        cost_estimate=pl.CostEstimate(
            flops=6 * depth * nx * ny * pick.shape[0],
            bytes_accessed=4 * depth * nx * (ny + pick.shape[0]),
            transcendentals=0,
        ),
    )(jnp.asarray(pick), second, third, field)


def depth_kernel(third_ref, one_ref, two_ref, out_ref, both_ref):
    rank, nx = out_ref.shape[1:]

    @pl.when(pl.program_id(0) == 0)
    def _():
        halves = [third_ref[:, 0, :, half * rank : (half + 1) * rank].reshape(-1, rank) for half in range(2)]
        high, low = split(jnp.concatenate(halves, 0).T)
        both_ref[:rank] = high
        both_ref[rank:] = low

    for g in range(out_ref.shape[0]):
        value = jnp.concatenate([ref[:, g].reshape(-1, nx) for ref in (one_ref, two_ref)], 0)
        out_ref[g] = product(both_ref[:rank], both_ref[...], value)


def depth_product(gathered, part, rank, groups):
    n, count, planes, nx = gathered.shape
    step = 2 if groups % 2 == 0 else 1
    block = (n, step, planes, nx)
    return pl.pallas_call(
        depth_kernel,
        grid=(groups // step,),
        in_specs=[
            pl.BlockSpec((n, 1, planes, nx), lambda i: (0, count - 1, 0, 0)),
            pl.BlockSpec(block, lambda i: (0, i, 0, 0)),
            pl.BlockSpec(block, lambda i: (0, groups // step + i, 0, 0)),
        ],
        out_specs=pl.BlockSpec((step, rank, nx), lambda i: (i, 0, 0)),
        out_shape=jax.ShapeDtypeStruct((groups, rank, nx), jnp.float32),
        scratch_shapes=[pltpu.VMEM((2 * rank, 2 * n * planes), jnp.bfloat16)],
        compiler_params=pltpu.CompilerParams(vmem_limit_bytes=VMEM_LIMIT),
        cost_estimate=pl.CostEstimate(
            flops=12 * n * groups * planes * nx * rank,
            bytes_accessed=8 * n * groups * planes * nx,
            transcendentals=0,
        ),
    )(gathered, part, part)


def shifts(moves, axis):
    n = lax.axis_size(axis)
    values = lax.optimization_barrier([value for value, _ in moves])
    return [
        lax.ppermute(value, axis, [(i, (i + by) % n) for i in range(n)])
        for value, (_, by) in zip(values, moves)
    ]


def ring_steps(parts, axis):
    n = len(parts)
    half = n // 2
    mid = parts[half].shape[0] // 2
    moving = shifts([(parts[half][:mid], 1), (parts[half][mid:], -1)], axis)
    for d in range(half - 1, 0, -1):
        up, down = yield moving
        if d == half - 1:
            up = jnp.concatenate([parts[d][:mid] + up, parts[d][mid:]], 0)
            down = jnp.concatenate([parts[n - d][:mid], parts[n - d][mid:] + down], 0)
        else:
            up = parts[d] + up
            down = parts[n - d] + down
        moving = shifts([(up, 1), (down, -1)], axis)
    up, down = yield moving
    yield parts[0] + up + down


def ring_sum(parts, axis):
    steps = ring_steps(parts, axis)
    value = next(steps)
    for _ in range(len(parts) // 2):
        value = steps.send(value)
    return value


def trade(value, axis):
    return lax.all_to_all(value, axis, 0, 0)


def spread(value, axis):
    n = lax.axis_size(axis)
    return trade(jnp.broadcast_to(value[None], (n,) + value.shape), axis)


def local(snapshot, basis_first, basis_second, basis_third):
    depth = snapshot.shape[0] * snapshot.shape[1]
    nx = snapshot.shape[2]
    ny = snapshot.shape[3]
    rank = basis_second.shape[1]
    gx = lax.axis_size("gx")
    gy = lax.axis_size("gy")
    vert = lax.axis_size("vert")
    share = rank // gy
    part_m = share // 2
    field = snapshot.reshape(depth, nx, ny)
    first = lax.dynamic_slice_in_dim(basis_first, lax.axis_index("gx") * nx, nx, 0)

    third = basis_third.reshape(depth, rank)

    def pick(pairs):
        return np.eye(rank, dtype=np.float32)[[place * share + within for place, within in pairs]]

    pick_f = pick([(place, part_m + v) for v in range(vert) for place in range(gy)])
    pick_m = pick([(place, within) for place in range(gy) for within in range(part_m)])

    half = depth // 2
    f, m1 = lead_product(pick_f, pick_m, basis_second, field, share, third)
    second, f = lax.optimization_barrier((basis_second, f))
    f = trade(f, "vert")

    m2 = mode_product(pick_m, second, field, share, half, half)
    m = [ring_sum([part[d * part_m : (d + 1) * part_m] for d in range(gy)], "gy") for part in (m1, m2)]
    m, f = lax.optimization_barrier((jnp.concatenate(m, 1), f))
    m = trade(m, "vert")

    parts = depth_product(f, f, rank, gy)
    ring = ring_steps([parts[d] for d in range(gy)], "gy")
    moving = next(ring)
    for _ in range(gy // 2 - 2):
        moving = ring.send(moving)
    moving, m = lax.optimization_barrier((moving, m))
    m = depth_product(f, m.reshape(vert, 2, half, nx), rank, 1)[0]
    f = ring.send(ring.send(moving))

    columns = jnp.concatenate([f, m], 0)
    weights = jnp.dot(columns, first, precision=HIGHEST)
    others = shifts([(weights, d) for d in range(1, gx)], "gx")
    for other in others:
        weights = weights + other
    updated = lax.dot_general(columns, weights, (((0,), (0,)), ((), ())), precision=HIGHEST)

    updated = jnp.sum(trade(updated.reshape(vert, nx // vert, rank), "vert"), axis=0)
    updated = jnp.sum(spread(updated, "gy"), axis=0) / float(rank * rank)
    return spread(updated, "vert").reshape(nx, rank)


def solution(mesh):
    placed = (P("vert", None, "gx", "gy"), P(), P("gy", None), P("vert", None, None))
    return jax.shard_map(
        local, mesh=mesh, in_specs=placed, out_specs=P("gx", None), check_vma=False
    )
```

```python
import functools

import jax
import jax.numpy as jnp
import numpy as np
from jax import lax
from jax.experimental import pallas as pl
from jax.experimental.pallas import tpu as pltpu
from jax.sharding import PartitionSpec as P

HIGHEST = lax.Precision.HIGHEST
NT = (((1,), (1,)), ((), ()))
NN = (((1,), (0,)), ((), ()))
VMEM_LIMIT = 14 * 2**20
STEP = 16
SETS = 8


def split(value):
    high = value.astype(jnp.bfloat16)
    return high, (value - high.astype(jnp.float32)).astype(jnp.bfloat16)


def product(high, both, value):
    rows = high.shape[0]
    v_high, v_low = split(value)
    main = lax.dot_general(both, v_high, NN, preferred_element_type=jnp.float32)
    rest = lax.dot_general(high, v_low, NN, preferred_element_type=jnp.float32)
    return main[:rows] + (main[rows:] + rest)


def mode_kernel(roll, first, pick_ref, second_ref, field_ref, out_ref, both_ref, held_ref, sems):
    rows = pick_ref.shape[0]
    ny = second_ref.shape[0]
    steps = held_ref.shape[0] // STEP
    now = pl.program_id(0)

    def fetch(i):
        return pltpu.make_async_copy(
            field_ref.at[pl.ds((first + i) * STEP, STEP)], held_ref.at[pl.ds(i * STEP, STEP)], sems.at[i]
        )

    @pl.when(now == 0)
    def _():
        for i in range(steps):
            fetch(i).start()
        pick = pltpu.roll(pick_ref[...], lax.axis_index("gy") * roll, 1).astype(jnp.bfloat16)
        both_ref[...] = jnp.zeros_like(both_ref)
        for part, value in enumerate(split(second_ref[...])):
            value = lax.dot_general(pick, value, NT, preferred_element_type=jnp.float32).astype(jnp.bfloat16)
            both_ref[part * rows : (part + 1) * rows, :ny] = value
            if part == 0:
                both_ref[:rows, ny:] = value

    fetch(now).wait()
    both = both_ref[...]
    for j in range(STEP):
        pair = jnp.concatenate(split(held_ref[now * STEP + j]), 1)
        value = lax.dot_general(both, pair, NT, preferred_element_type=jnp.float32)
        out_ref[:, j, :] = value[:rows] + value[rows:]


def mode_product(pick, second, field, roll, start, count):
    _, nx, ny = field.shape
    steps = count // STEP
    rows = pick.shape[0]
    return pl.pallas_call(
        functools.partial(mode_kernel, roll, start // STEP),
        grid=(steps,),
        in_specs=[
            pl.BlockSpec(pick.shape, lambda i: (0, 0)),
            pl.BlockSpec(second.shape, lambda i: (0, 0)),
            pl.BlockSpec(memory_space=pl.ANY),
        ],
        out_specs=pl.BlockSpec((rows, STEP, nx), lambda i: (0, i, 0)),
        out_shape=jax.ShapeDtypeStruct((rows, count, nx), jnp.float32),
        scratch_shapes=[
            pltpu.VMEM((2 * rows, 2 * ny), jnp.bfloat16),
            pltpu.VMEM((count, nx, ny), jnp.float32),
            pltpu.SemaphoreType.DMA((steps,)),
        ],
        compiler_params=pltpu.CompilerParams(vmem_limit_bytes=46 * 2**20),
        cost_estimate=pl.CostEstimate(
            flops=6 * count * nx * ny * rows,
            bytes_accessed=4 * count * nx * (ny + rows),
            transcendentals=0,
        ),
    )(jnp.asarray(pick), second, field)


def lead_kernel(
    roll, pick_ref, second_ref, third_ref, field_ref, f_ref, m_ref, both_ref, held_ref, stage_ref, pack_ref, sems, out_sems, third_sem
):
    rows = pick_ref.shape[0] // 2
    ny = second_ref.shape[0]
    rank = third_ref.shape[1]
    steps = held_ref.shape[0] // STEP
    sets = f_ref.shape[0]
    groups = rows // sets
    per_half = steps // 2
    now = pl.program_id(0)

    def fetch(i):
        return pltpu.make_async_copy(
            field_ref.at[pl.ds(i * STEP, STEP)], held_ref.at[pl.ds(i * STEP, STEP)], sems.at[i]
        )

    def send(i):
        plane = pl.multiple_of(i % per_half * STEP, STEP)
        target = f_ref.at[:, pl.ds(i // per_half * groups, groups), pl.ds(plane, STEP), :]
        return pltpu.make_async_copy(stage_ref.at[i % 2], target, out_sems.at[i % 2])

    def send_third(v):
        return pltpu.make_async_copy(pack_ref, f_ref.at[v, 2 * groups], third_sem.at[v])

    @pl.when(now == 0)
    def _():
        for i in range(steps):
            fetch(i).start()
        for half in range(2):
            pack_ref[:, half * rank : (half + 1) * rank] = third_ref[half * per_half * STEP : (half + 1) * per_half * STEP, :]
        for v in range(sets):
            send_third(v).start()
        pick = pltpu.roll(pick_ref[...], lax.axis_index("gy") * roll, 1).astype(jnp.bfloat16)
        both_ref[...] = jnp.zeros_like(both_ref)
        for part, value in enumerate(split(second_ref[...])):
            value = lax.dot_general(pick, value, NT, preferred_element_type=jnp.float32).astype(jnp.bfloat16)
            for n in range(2):
                place = (2 * n + part) * rows
                both_ref[place : place + rows, :ny] = value[n * rows : (n + 1) * rows]
                if part == 0:
                    both_ref[place : place + rows, ny:] = value[n * rows : (n + 1) * rows]

    @pl.when(now >= 2)
    def _():
        send(now - 2).wait()

    fetch(now).wait()

    def multiply(with_m):
        both = both_ref[...] if with_m else both_ref[: 2 * rows]
        for j in range(STEP):
            pair = jnp.concatenate(split(held_ref[now * STEP + j]), 1)
            value = lax.dot_general(both, pair, NT, preferred_element_type=jnp.float32)
            f = value[:rows] + value[rows : 2 * rows]
            for v in range(sets):
                stage_ref[now % 2, v, :, j, :] = f[v * groups : (v + 1) * groups]
            if with_m:
                m_ref[:, j, :] = value[2 * rows : 3 * rows] + value[3 * rows :]

    @pl.when(now < per_half)
    def _():
        multiply(True)

    @pl.when(now >= per_half)
    def _():
        multiply(False)

    send(now).start()

    @pl.when(now == steps - 1)
    def _():
        send(now - 1).wait()
        send(now).wait()
        for v in range(sets):
            send_third(v).wait()


def lead_product(pick_f, pick_m, second, field, roll, third):
    depth, nx, ny = field.shape
    steps = depth // STEP
    pick = np.concatenate([pick_f, pick_m], 0)
    rows = pick_f.shape[0]
    groups = rows // SETS
    return pl.pallas_call(
        functools.partial(lead_kernel, roll),
        grid=(steps,),
        in_specs=[
            pl.BlockSpec(pick.shape, lambda i: (0, 0)),
            pl.BlockSpec(second.shape, lambda i: (0, 0)),
            pl.BlockSpec(third.shape, lambda i: (0, 0)),
            pl.BlockSpec(memory_space=pl.ANY),
        ],
        out_specs=[
            pl.BlockSpec(memory_space=pl.ANY),
            pl.BlockSpec((rows, STEP, nx), lambda i: (0, jnp.minimum(i, steps // 2 - 1), 0)),
        ],
        out_shape=[
            jax.ShapeDtypeStruct((SETS, 2 * groups + 1, depth // 2, nx), jnp.float32),
            jax.ShapeDtypeStruct((rows, depth // 2, nx), jnp.float32),
        ],
        scratch_shapes=[
            pltpu.VMEM((4 * rows, 2 * ny), jnp.bfloat16),
            pltpu.VMEM((depth, nx, ny), jnp.float32),
            pltpu.VMEM((2, SETS, groups, STEP, nx), jnp.float32),
            pltpu.VMEM((depth // 2, nx), jnp.float32),
            pltpu.SemaphoreType.DMA((steps,)),
            pltpu.SemaphoreType.DMA((2,)),
            pltpu.SemaphoreType.DMA((SETS,)),
        ],
        compiler_params=pltpu.CompilerParams(vmem_limit_bytes=54 * 2**20),
        cost_estimate=pl.CostEstimate(
            flops=6 * depth * nx * ny * pick.shape[0],
            bytes_accessed=4 * depth * nx * (ny + pick.shape[0]),
            transcendentals=0,
        ),
    )(jnp.asarray(pick), second, third, field)


def depth_kernel(third_ref, one_ref, two_ref, out_ref, both_ref):
    rank, nx = out_ref.shape[1:]

    @pl.when(pl.program_id(0) == 0)
    def _():
        halves = [third_ref[:, 0, :, half * rank : (half + 1) * rank].reshape(-1, rank) for half in range(2)]
        high, low = split(jnp.concatenate(halves, 0).T)
        both_ref[:rank] = high
        both_ref[rank:] = low

    for g in range(out_ref.shape[0]):
        value = jnp.concatenate([ref[:, g].reshape(-1, nx) for ref in (one_ref, two_ref)], 0)
        out_ref[g] = product(both_ref[:rank], both_ref[...], value)


def depth_product(gathered, part, rank, groups):
    n, count, planes, nx = gathered.shape
    step = 4 if groups % 4 == 0 else 1
    block = (n, step, planes, nx)
    return pl.pallas_call(
        depth_kernel,
        grid=(groups // step,),
        in_specs=[
            pl.BlockSpec((n, 1, planes, nx), lambda i: (0, count - 1, 0, 0)),
            pl.BlockSpec(block, lambda i: (0, i, 0, 0)),
            pl.BlockSpec(block, lambda i: (0, groups // step + i, 0, 0)),
        ],
        out_specs=pl.BlockSpec((step, rank, nx), lambda i: (i, 0, 0)),
        out_shape=jax.ShapeDtypeStruct((groups, rank, nx), jnp.float32),
        scratch_shapes=[pltpu.VMEM((2 * rank, 2 * n * planes), jnp.bfloat16)],
        compiler_params=pltpu.CompilerParams(vmem_limit_bytes=VMEM_LIMIT),
        cost_estimate=pl.CostEstimate(
            flops=12 * n * groups * planes * nx * rank,
            bytes_accessed=8 * n * groups * planes * nx,
            transcendentals=0,
        ),
    )(gathered, part, part)


def shifts(moves, axis):
    n = lax.axis_size(axis)
    values = lax.optimization_barrier([value for value, _ in moves])
    return [
        lax.ppermute(value, axis, [(i, (i + by) % n) for i in range(n)])
        for value, (_, by) in zip(values, moves)
    ]


def ring_steps(parts, axis):
    n = len(parts)
    half = n // 2
    mid = parts[half].shape[0] // 2
    moving = shifts([(parts[half][:mid], 1), (parts[half][mid:], -1)], axis)
    for d in range(half - 1, 0, -1):
        up, down = yield moving
        if d == half - 1:
            up = jnp.concatenate([parts[d][:mid] + up, parts[d][mid:]], 0)
            down = jnp.concatenate([parts[n - d][:mid], parts[n - d][mid:] + down], 0)
        else:
            up = parts[d] + up
            down = parts[n - d] + down
        moving = shifts([(up, 1), (down, -1)], axis)
    up, down = yield moving
    yield parts[0] + up + down


def ring_sum(parts, axis):
    steps = ring_steps(parts, axis)
    value = next(steps)
    for _ in range(len(parts) // 2):
        value = steps.send(value)
    return value


def trade(value, axis):
    return lax.all_to_all(value, axis, 0, 0)


def spread(value, axis):
    n = lax.axis_size(axis)
    return trade(jnp.broadcast_to(value[None], (n,) + value.shape), axis)


def local(snapshot, basis_first, basis_second, basis_third):
    depth = snapshot.shape[0] * snapshot.shape[1]
    nx = snapshot.shape[2]
    ny = snapshot.shape[3]
    rank = basis_second.shape[1]
    gx = lax.axis_size("gx")
    gy = lax.axis_size("gy")
    vert = lax.axis_size("vert")
    share = rank // gy
    part_m = share // 2
    field = snapshot.reshape(depth, nx, ny)
    first = lax.dynamic_slice_in_dim(basis_first, lax.axis_index("gx") * nx, nx, 0)

    third = basis_third.reshape(depth, rank)

    def pick(pairs):
        return np.eye(rank, dtype=np.float32)[[place * share + within for place, within in pairs]]

    pick_f = pick([(place, part_m + v) for v in range(vert) for place in range(gy)])
    pick_m = pick([(place, within) for place in range(gy) for within in range(part_m)])

    half = depth // 2
    f, m1 = lead_product(pick_f, pick_m, basis_second, field, share, third)
    second, f = lax.optimization_barrier((basis_second, f))
    f = trade(f, "vert")

    m2 = mode_product(pick_m, second, field, share, half, half)
    m = [ring_sum([part[d * part_m : (d + 1) * part_m] for d in range(gy)], "gy") for part in (m1, m2)]
    m, f = lax.optimization_barrier((jnp.concatenate(m, 1), f))
    m = trade(m, "vert")

    parts = depth_product(f, f, rank, gy)
    ring = ring_steps([parts[d] for d in range(gy)], "gy")
    moving = next(ring)
    for _ in range(gy // 2 - 2):
        moving = ring.send(moving)
    moving, m = lax.optimization_barrier((moving, m))
    m = depth_product(f, m.reshape(vert, 2, half, nx), rank, 1)[0]
    f = ring.send(ring.send(moving))

    columns = jnp.concatenate([f, m], 0)
    weights = jnp.dot(columns, first, precision=HIGHEST)
    others = shifts([(weights, d) for d in range(1, gx)], "gx")
    for other in others:
        weights = weights + other
    updated = lax.dot_general(columns, weights, (((0,), (0,)), ((), ())), precision=HIGHEST)

    updated = jnp.sum(trade(updated.reshape(vert, nx // vert, rank), "vert"), axis=0)
    updated = jnp.sum(spread(updated, "gy"), axis=0) / float(rank * rank)
    return spread(updated, "vert").reshape(nx, rank)


def solution(mesh):
    placed = (P("vert", None, "gx", "gy"), P(), P("gy", None), P("vert", None, None))
    return jax.shard_map(
        local, mesh=mesh, in_specs=placed, out_specs=P("gx", None), check_vma=False
    )
```
